128 devices in a mesh: pix: 8 (over x, core), mz: 16 (over z, y).
Axes of the slice: x: 4, y: 4, z: 4, core: 2. Of those that a mesh axis runs over, the one named last changes fastest.
Arguments:
- spectra: bfloat16 [256, 1024, 256], P('pix', 'mz'), may hold values from -40 to 40
- owner: int32 [384], replicated, may hold values from 0 to 15, as said below
- peaks: int32 [384, 4], replicated, may hold values from 0 to 255, as said below
- pattern_index: int32 [384], replicated, may hold values from 0 to 63
- patterns: float32 [64, 4], replicated, may hold values from 0.05 to 1
Outputs:
- ion_images: bfloat16 [256, 256, 1024], P('mz', 'pix')
- formula_images: bfloat16 [768, 256, 1024], P('mz', 'pix')
- chaos: float32 [768], P('mz')
The draws below stay inside these ranges and needn't reach their ends.
Inputs may be any that keep to these rules, and one draw needn't show every extreme that they name: Each of the 16 owners has at most 48 formulas, and some owner has exactly 48. `peaks`: each formula's 4 bins rise strictly by equal steps of 1 to 4 bins.
All inputs are finite; a program needn't handle non-finite values.
Results may differ from the reference program's by a relative error of at most 0.0056.
Values may be sent and summed in bfloat16 or wider, within the bound.
A program may use at most 128 MiB of HBM per device.

```python
import math
import jax
import jax.numpy as jnp
from jax import lax

B = 256
W = 1024
CAP = 48
P_SIZE = 64
PEAKS = 4
H = 256
FORMULAS = 384
SLOTS = 768
N_MZ = 16


def draw_spectra(key, part):
    key = jax.random.fold_in(key, 11)
    noise_key, column_key = jax.random.split(key)
    row_scale = 10.0 ** (0.5 * jnp.arange(H, dtype=jnp.float32) / H)
    column_scale = 10.0 ** (0.5 * jax.random.uniform(column_key, (W,), dtype=jnp.float32))
    base = jnp.clip(jax.random.normal(noise_key, (H, W, B), dtype=jnp.float32), -4.0, 4.0)
    return (base * row_scale[:, None, None] * column_scale[None, :, None]).astype(jnp.bfloat16)


def draw_owner(key, part):
    key = jax.random.fold_in(key, 12)
    perm_key, shuffle_key = jax.random.split(key)
    profile = jnp.array([CAP, CAP // 2, CAP // 4, CAP // 4], dtype=jnp.int32)
    counts = jnp.tile(profile, N_MZ // 4)
    ends = jnp.cumsum(counts).astype(jnp.int32)
    position = jnp.arange(FORMULAS, dtype=jnp.int32)
    rank_of = jnp.sum((position[:, None] >= ends[None, :]).astype(jnp.int32), axis=1)
    order = jax.random.permutation(perm_key, N_MZ).astype(jnp.int32)
    sorted_owner = order[rank_of]
    return jax.random.permutation(shuffle_key, sorted_owner).astype(jnp.int32)


def draw_peaks(key, part):
    key = jax.random.fold_in(key, 13)
    first_key, step_key = jax.random.split(key)
    first = jax.random.randint(first_key, (FORMULAS, 1), 0, B - 12, dtype=jnp.int32)
    spacing = jax.random.randint(step_key, (FORMULAS, 1), 1, 5, dtype=jnp.int32)
    return (first + spacing * jnp.arange(PEAKS, dtype=jnp.int32)[None, :]).astype(jnp.int32)


def place_ends(values, own_key, smallest, largest):
    place = [jax.random.randint(jax.random.fold_in(own_key, axis), (), 0, length) for axis, length in enumerate(values.shape)]
    main_axis = values.shape.index(max(values.shape))
    neighbour = place[:main_axis] + [(place[main_axis] + 1) % values.shape[main_axis]] + place[main_axis + 1:]
    return values.at[tuple(place)].set(smallest).at[tuple(neighbour)].set(largest)


def setup_inputs(seed: int = 0) -> dict:
    streams_of = jax.random.split(jax.random.key(seed), 6)
    spectra = draw_spectra(jax.random.fold_in(streams_of[5], 71), 0)
    owner = draw_owner(jax.random.fold_in(streams_of[5], 71), 0)
    peaks = draw_peaks(jax.random.fold_in(streams_of[5], 71), 0)
    pattern_index = place_ends(jax.random.randint(streams_of[3], (FORMULAS,), 0, P_SIZE), jax.random.fold_in(streams_of[3], 1), 0, P_SIZE - 1).astype(jnp.int32)
    patterns = jnp.clip(jnp.exp(jax.random.uniform(streams_of[4], (P_SIZE, PEAKS), jnp.float32, math.log(0.05), math.log(1.0))), 0.05, 1.0)
    return {"spectra": spectra, "owner": owner, "peaks": peaks, "pattern_index": pattern_index, "patterns": patterns}


gauss_raw = [math.exp(-offset * offset / 4.5) for offset in range(-3, 4)]
gauss_taps = [entry_value / sum(gauss_raw) for entry_value in gauss_raw]


def blur_axis(padded, axis, count):
    total = gauss_taps[0] * lax.slice_in_dim(padded, 0, count, axis=axis)
    for offset in range(1, len(gauss_taps)):
        total = total + gauss_taps[offset] * lax.slice_in_dim(padded, offset, offset + count, axis=axis)
    return total


def slot_coefficients(owner, peaks, pattern_index, patterns, slots, bins, owners_count):
    owner_hot = (owner[:, None] == jnp.arange(owners_count)[None, :]).astype(jnp.int32)
    earlier = (jnp.cumsum(owner_hot, axis=0) - owner_hot).astype(jnp.int32)
    rank_in = jnp.sum(earlier * owner_hot, axis=1).astype(jnp.int32)
    slot_of = owner * (slots // owners_count) + rank_in
    pattern_hot = (pattern_index[:, None] == jnp.arange(patterns.shape[0])[None, :]).astype(jnp.float32)
    peak_weight = jnp.dot(pattern_hot, patterns, precision=lax.Precision.HIGHEST)
    peak_hot = (peaks[:, :, None] == jnp.arange(bins)[None, None, :]).astype(jnp.float32)
    per_formula = jnp.einsum("fk,fkb->fb", peak_weight, peak_hot, precision=lax.Precision.HIGHEST)
    slot_hot = (jnp.arange(slots)[:, None] == slot_of[None, :]).astype(jnp.float32)
    return jnp.dot(slot_hot, per_formula, precision=lax.Precision.HIGHEST).astype(jnp.bfloat16)


def chaos_scores(images):
    values = images.astype(jnp.float32)
    across = values[:, :, 1:] - values[:, :, :-1]
    down = values[:, 1:, :] - values[:, :-1, :]
    rough = jnp.sum(across * across, axis=(1, 2)) + jnp.sum(down * down, axis=(1, 2))
    energy = jnp.sum(values * values, axis=(1, 2))
    return rough / (energy + 1e-5)


def reference(spectra, owner, peaks, pattern_index, patterns):
    images = jnp.transpose(spectra, (2, 0, 1)).astype(jnp.float32)
    padded = jnp.pad(images, ((0, 0), (3, 3), (3, 3)))
    rows_done = blur_axis(padded, 1, images.shape[1])
    ion_images = blur_axis(rows_done, 2, images.shape[2]).astype(jnp.bfloat16)
    coef = slot_coefficients(owner, peaks, pattern_index, patterns, SLOTS, B, N_MZ)
    flat = jnp.dot(coef, ion_images.reshape(B, H * W), preferred_element_type=jnp.float32)
    formula_images = flat.reshape(SLOTS, H, W).astype(jnp.bfloat16)
    chaos = chaos_scores(formula_images)
    return ion_images, formula_images, chaos
```

```python
import math

import jax
import jax.numpy as jnp
import ml_dtypes
import numpy as np
from jax import lax
from jax.experimental import pallas as pl
from jax.experimental.pallas import tpu as pltpu
from jax.sharding import PartitionSpec as P

MESH = pl.DeviceIdType.MESH
F32, BF16 = jnp.float32, jnp.bfloat16

CAP = 48
N_MZ, N_PIX = 16, 8
SIDE = 4
ROWS, COLS, BINS = 32, 64, 256
GROUPS = ROWS // 4
PIXELS = ROWS * COLS
EXTRA = 128
TILES = (PIXELS + EXTRA) // 128
PARTS = 4

gauss_raw = [math.exp(-offset * offset / 4.5) for offset in range(-3, 4)]
taps = [value / sum(gauss_raw) for value in gauss_raw]

ORDER = [(0, 1), (1, 0), (0, 3), (3, 0), (1, 1), (3, 3), (1, 3), (3, 1), (2, 0), (0, 2), (2, 1), (1, 2), (2, 3), (3, 2), (2, 2)]


def tap(offset):
    return taps[offset + 3] if -3 <= offset <= 3 else 0.0


def split(matrix):
    high = matrix.astype(ml_dtypes.bfloat16)
    low = (matrix - high.astype(np.float64)).astype(ml_dtypes.bfloat16)
    return high, low


def constants():
    own = np.zeros((256, 256))
    sides = np.zeros((256, 32))
    pick = np.zeros((32, 256))
    for r in range(4):
        for c in range(COLS):
            for k in range(COLS):
                own[r * COLS + c, r * COLS + k] = tap(k - c)
            for j in range(4):
                sides[r * COLS + c, r * 4 + j] = tap(j - 4 - c)
                sides[r * COLS + c, 16 + r * 4 + j] = tap(COLS + j - c)
        for j in range(4):
            pick[r * 4 + j, r * COLS + j] = 1.0
            pick[16 + r * 4 + j, r * COLS + COLS - 4 + j] = 1.0
    seam = np.zeros((64, 320))
    for r in range(ROWS):
        for k in range(ROWS + 8):
            down = tap(k - 4 - r)
            for j in range(4):
                for edge in range(2):
                    seam[edge * 32 + r, k * 4 + j] = down * tap(j - 4 + 1 - edge)
                    seam[edge * 32 + r, 160 + k * 4 + j] = down * tap(j + 1 - edge)
    own_high, own_low = split(own)
    sides_high, sides_low = split(sides)
    blank = np.zeros((256, 64), ml_dtypes.bfloat16)
    first = np.concatenate([own_high, own_low, sides_high, sides_low, blank], axis=1)
    seam_high, seam_low = split(seam)
    second = np.zeros((96, 640), ml_dtypes.bfloat16)
    second[:64] = np.concatenate([seam_high, seam_low], axis=1)
    second[64:, :256] = pick.astype(ml_dtypes.bfloat16)
    return first, second


def dot(a, b):
    return jnp.dot(a, b, preferred_element_type=F32)


def dot_nt(a, b):
    return lax.dot_general(a, b, (((1,), (1,)), ((), ())), preferred_element_type=F32)


def iota(shape, axis):
    return lax.broadcasted_iota(jnp.int32, shape, axis)


def produce_kernel(
    spectra, owner, peaks, pattern_index, patterns, blur, more, parts, score,
    xs, pack_left, pack_right, left, right, ys, ion, coef, form, out, note, notes, total, totals,
    load_sem, halo_send, halo_recv, part_send, part_recv, part_own, note_send, note_recv, total_send, total_recv,
):
    pix, mz = lax.axis_index("pix"), lax.axis_index("mz")
    z, y = mz // SIDE, mz % SIDE

    def device(dp, dm):
        return {"pix": (pix + dp + N_PIX) % N_PIX, "mz": (mz + dm + N_MZ) % N_MZ}

    def peer(dz, dy):
        return ((z + dz) % SIDE) * SIDE + (y + dy) % SIDE

    def remote(src, dst, send, recv, target):
        return pltpu.make_async_remote_copy(
            src_ref=src, dst_ref=dst, send_sem=send, recv_sem=recv, device_id=target, device_id_type=MESH
        )

    load = pltpu.make_async_copy(spectra, xs.at[pl.ds(1, GROUPS)], load_sem)
    load.start()

    barrier = pltpu.get_barrier_semaphore()
    near = [(0, 1), (0, -1), (1, 0), (-1, 0), (1, 1), (1, -1), (-1, 1), (-1, -1)]
    for dp, dm in near[2:]:
        pl.semaphore_signal(barrier, inc=1, device_id=device(dp, dm), device_id_type=MESH)
    for dz, dy in ORDER:
        pl.semaphore_signal(barrier, inc=1, device_id={"mz": peer(dz, dy)}, device_id_type=MESH)
    for dp in range(2, N_PIX - 1):
        pl.semaphore_signal(barrier, inc=1, device_id=device(dp, 0), device_id_type=MESH)

    load.wait()
    pick = more[64:96, 0:256]

    def pack(g, carry):
        ends = dot(pick, xs[g]).astype(BF16)
        pack_left[g] = ends[0:16]
        pack_right[g] = ends[16:32]
        return carry

    lax.fori_loop(1, GROUPS + 1, pack, 0)
    pl.semaphore_wait(barrier, 6 + len(ORDER) + N_PIX - 3)

    inner = pl.ds(1, GROUPS)
    halo = [
        (xs.at[GROUPS], xs.at[0], (1, 0)),
        (xs.at[1], xs.at[GROUPS + 1], (-1, 0)),
        (pack_right.at[inner], left.at[inner], (0, 1)),
        (pack_left.at[inner], right.at[inner], (0, -1)),
        (pack_right.at[GROUPS], left.at[0], (1, 1)),
        (pack_right.at[1], left.at[GROUPS + 1], (-1, 1)),
        (pack_left.at[GROUPS], right.at[0], (1, -1)),
        (pack_left.at[1], right.at[GROUPS + 1], (-1, -1)),
    ]
    halo = [
        remote(src, dst, halo_send.at[i], halo_recv.at[i], device(*to)) for i, (src, dst, to) in enumerate(halo)
    ]
    for copy in halo:
        copy.start()

    blur_high, blur_low, blur_sides = blur[:, 0:256], blur[:, 256:512], blur[:, 512:576]

    def columns_own(g, carry):
        x = xs[g]
        ys[g] = dot(blur_high, x) + dot(blur_low, x)
        return carry

    lax.fori_loop(1, GROUPS + 1, columns_own, 0)

    count = owner.shape[1]
    owner_hot = (iota((N_MZ, count), 0) == owner[...]).astype(F32)
    before = (iota((count, count), 0) < iota((count, count), 1)).astype(F32).astype(BF16)
    earlier = dot(owner_hot.astype(BF16), before)
    rank = jnp.sum(earlier * owner_hot, axis=0, keepdims=True)
    slot = owner[...] * CAP + rank.astype(jnp.int32)
    pattern_hot = (iota((patterns.shape[1], count), 0) == pattern_index[...]).astype(F32).astype(BF16)
    weight = dot(patterns[...].astype(BF16), pattern_hot)
    spread = jnp.zeros((BINS, count), F32)
    for k in range(peaks.shape[0]):
        spread += jnp.where(iota((BINS, count), 0) == peaks[k : k + 1, :], weight[k : k + 1, :], 0.0)
    spread = spread.astype(BF16)
    place = iota((256, count), 0)
    place = (place // 16) * CAP + place % 16
    coef[0] = (iota((256, BINS), 0) == iota((256, BINS), 1)).astype(F32).astype(BF16)
    for q in range(1, PARTS):
        slot_hot = (place + (q - 1) * 16 == slot).astype(F32).astype(BF16)
        coef[q] = dot_nt(slot_hot, spread).astype(BF16)

    for copy in halo:
        copy.wait()

    @pl.when(pix == 0)
    def _():
        xs[0] = jnp.zeros(xs.shape[1:], BF16)
        left[0] = jnp.zeros(left.shape[1:], BF16)
        right[0] = jnp.zeros(right.shape[1:], BF16)

    @pl.when(pix == N_PIX - 1)
    def _():
        xs[GROUPS + 1] = jnp.zeros(xs.shape[1:], BF16)
        left[GROUPS + 1] = jnp.zeros(left.shape[1:], BF16)
        right[GROUPS + 1] = jnp.zeros(right.shape[1:], BF16)

    @pl.when(mz == 0)
    def _():
        left[...] = jnp.zeros(left.shape, BF16)

    @pl.when(mz == N_MZ - 1)
    def _():
        right[...] = jnp.zeros(right.shape, BF16)

    columns_own(0, 0)
    columns_own(GROUPS + 1, 0)

    def columns_sides(g, carry):
        sides = jnp.concatenate([left[g], right[g], left[g], right[g]], axis=0)
        ys[g] += dot(blur_sides, sides)
        return carry

    lax.fori_loop(0, GROUPS + 2, columns_sides, 0)

    for g in (0, GROUPS + 1):
        pack_left[g] = dot(pick[0:16], xs[g]).astype(BF16)
    edge = jnp.concatenate([left[...].reshape(160, BINS), pack_left[...].reshape(160, BINS)], axis=0)
    ion[PIXELS + 64 : PIXELS + 128] = (dot(more[0:64, 0:320], edge) + dot(more[0:64, 320:640], edge)).astype(BF16)

    def row(k, first):
        result = taps[3] * first(k + 3)
        for i in range(3):
            result = result + taps[i] * (first(k + i) + first(k + 6 - i))
        return result

    def slab(k):
        return ys[k // 4, pl.ds(pl.multiple_of((k % 4) * COLS, COLS), COLS), :]

    def rows(r, carry):
        at = pl.multiple_of((r % 16) * 128 + (r // 16) * 64, 64)
        ion[pl.ds(at, COLS), :] = row(r + 1, slab).astype(BF16)
        return carry

    lax.fori_loop(0, ROWS, rows, 0)
    ion[PIXELS : PIXELS + 64] = row(0, slab).astype(BF16)

    def product(q):
        def tile(n, carry):
            at = pl.multiple_of(n * 256, 256)
            result = dot_nt(coef[q], ion[pl.ds(at, 256), :])
            form[q, pl.ds(pl.multiple_of(n * 512, 512), 256), :] = result[:, 0:128]
            form[q, pl.ds(pl.multiple_of(n * 512 + 256, 256), 256), :] = result[:, 128:256]
            return carry

        lax.fori_loop(0, PIXELS // 256, tile, 0)
        form[q, pl.ds(PIXELS * 2, 256), :] = dot_nt(coef[q], ion[pl.ds(PIXELS, 128), :])

        def turn(d, carry):
            for s in range(16):
                out[q, d, s] = form[q, pl.ds(d * 16 + s, 16, stride=256), :].astype(BF16)
            return carry

        lax.fori_loop(0, N_MZ, turn, 0)

    def send(q):
        copies = []
        for i, (dz, dy) in enumerate(ORDER):
            to = peer(dz, dy)
            copies.append(
                remote(out.at[q, to], parts.at[q, mz], part_send.at[q, i], part_recv.at[q, i], {"mz": to})
            )
        copies.append(pltpu.make_async_copy(out.at[q, mz], parts.at[q, mz], part_own.at[q]))
        for copy in copies:
            copy.start()
        return copies

    product(0)
    copies = send(0)
    product(1)
    copies += send(1)
    product(2)
    product(3)

    lane, sub = iota((8, 128), 1), iota((8, 128), 0)
    keep_across = (lane % 64 != 0).astype(F32)
    keep_seam = jnp.where(mz > 0, (lane >= 96).astype(F32), 0.0)
    keep_top = jnp.where(pix > 0, 1.0, jnp.where(lane < 64, 0.0, 1.0))
    note[...] = jnp.zeros(note.shape, F32)

    for q in range(1, PARTS):
        def scores(d, carry, q=q):
            acc = jnp.zeros((8, 128), F32)
            for half in range(2):
                def value(j):
                    at = pl.multiple_of(j * 256 + d * 16 + half * 8, 8)
                    return form[q, pl.ds(at, 8), :].astype(BF16).astype(F32)

                extra = value(TILES - 1)
                prior = jnp.where(lane < 64, extra, pltpu.roll(value(15), 64, 1))
                across = jnp.zeros((8, 128), F32)
                down = jnp.zeros((8, 128), F32)
                energy = jnp.zeros((8, 128), F32)
                for j in range(16):
                    now = value(j)
                    step = now - pltpu.roll(now, 1, 1)
                    across += step * step
                    step = now - prior
                    if j == 0:
                        step = step * keep_top
                    down += step * step
                    energy += now * now
                    prior = now
                step = extra - pltpu.roll(extra, 32, 1)
                rough = across * keep_across + down + step * step * keep_seam
                rough = jnp.sum(rough, axis=1, keepdims=True)
                energy = jnp.sum(energy, axis=1, keepdims=True)
                base = (q - 1) * 16 + half * 8
                acc += jnp.where(lane == sub + base, rough, 0.0) + jnp.where(lane == sub + base + 64, energy, 0.0)
            note[d] += acc
            return carry

        lax.fori_loop(0, N_MZ, scores, 0)

    small = []
    for i, (dz, dy) in enumerate(ORDER):
        to = peer(dz, dy)
        small.append(remote(note.at[to], notes.at[mz], note_send.at[i], note_recv.at[i], {"mz": to}))
    for copy in small:
        copy.start()
    copies += send(2)
    for copy in small:
        copy.wait()
    notes[mz] = note[mz]
    total[...] = jnp.sum(notes[...], axis=0)
    small = []
    for dp in range(1, N_PIX):
        to = device(dp, 0)
        small.append(remote(total, totals.at[pix], total_send.at[dp], total_recv.at[dp], to))
    for copy in small:
        copy.start()
    copies += send(3)
    for copy in small:
        copy.wait()
    totals[pix] = total[...]
    final = jnp.sum(jnp.sum(totals[...], axis=0), axis=0, keepdims=True)
    final = final / (pltpu.roll(final, 64, 1) + 1e-5)
    score[...] = jnp.broadcast_to(final, (8, 128))
    for copy in copies:
        copy.wait()


def place_kernel(parts, score, ion_out, form_out, chaos_out):
    step = pl.program_id(0)

    def fill(target):
        def one(s, carry):
            for j in range(N_MZ // 2):
                a, b = parts[0, 2 * j, s], parts[0, 2 * j + 1, s]
                at = slice(j * 128, (j + 1) * 128)
                target[s, 0:16, at] = jnp.concatenate([a[:, :64], b[:, :64]], axis=1)
                target[s, 16:32, at] = jnp.concatenate([a[:, 64:], b[:, 64:]], axis=1)
            return carry

        lax.fori_loop(0, 16, one, 0)

    @pl.when(step == 0)
    def _():
        fill(ion_out)
        chaos_out[...] = score[...]

    @pl.when(step > 0)
    def _():
        fill(form_out)


def body(spectra, owner, peaks, pattern_index, patterns):
    first, second = constants()
    vmem = pl.BlockSpec(memory_space=pltpu.VMEM)
    hbm = pl.BlockSpec(memory_space=pl.ANY)
    dma = pltpu.SemaphoreType.DMA
    peers = len(ORDER)
    parts, score = pl.pallas_call(
        produce_kernel,
        out_shape=(
            jax.ShapeDtypeStruct((PARTS, N_MZ, 16, 16, 128), BF16),
            jax.ShapeDtypeStruct((8, 128), F32),
        ),
        in_specs=[hbm] + [vmem] * 6,
        out_specs=(hbm, vmem),
        scratch_shapes=[
            pltpu.VMEM((GROUPS + 2, 256, BINS), BF16),
            pltpu.VMEM((GROUPS + 2, 16, BINS), BF16),
            pltpu.VMEM((GROUPS + 2, 16, BINS), BF16),
            pltpu.VMEM((GROUPS + 2, 16, BINS), BF16),
            pltpu.VMEM((GROUPS + 2, 16, BINS), BF16),
            pltpu.VMEM((GROUPS + 2, 256, BINS), F32),
            pltpu.VMEM((PIXELS + EXTRA, BINS), BF16),
            pltpu.VMEM((PARTS, 256, BINS), BF16),
            pltpu.VMEM((PARTS, TILES * 256, 128), F32),
            pltpu.VMEM((PARTS, N_MZ, 16, 16, 128), BF16),
            pltpu.VMEM((N_MZ, 8, 128), F32),
            pltpu.VMEM((N_MZ, 8, 128), F32),
            pltpu.VMEM((8, 128), F32),
            pltpu.VMEM((N_PIX, 8, 128), F32),
            dma,
            dma((8,)),
            dma((8,)),
            dma((PARTS, peers)),
            dma((PARTS, peers)),
            dma((PARTS,)),
            dma((peers,)),
            dma((peers,)),
            dma((N_PIX,)),
            dma((N_PIX,)),
        ],
        compiler_params=pltpu.CompilerParams(
            collective_id=0, has_side_effects=True, vmem_limit_bytes=48 * 2**20
        ),
    )(
        spectra.reshape(GROUPS, 256, BINS),
        owner.reshape(1, -1),
        peaks.T,
        pattern_index.reshape(1, -1),
        patterns.T,
        jnp.asarray(first),
        jnp.asarray(second),
    )
    ion_images, formula_images, chaos = pl.pallas_call(
        place_kernel,
        grid=(PARTS,),
        out_shape=(
            jax.ShapeDtypeStruct((16, ROWS, COLS * N_MZ), BF16),
            jax.ShapeDtypeStruct((CAP, ROWS, COLS * N_MZ), BF16),
            jax.ShapeDtypeStruct((8, 128), F32),
        ),
        in_specs=[
            pl.BlockSpec((1, N_MZ, 16, 16, 128), lambda i: (i, 0, 0, 0, 0)),
            pl.BlockSpec((8, 128), lambda i: (0, 0)),
        ],
        out_specs=(
            pl.BlockSpec((16, ROWS, COLS * N_MZ), lambda i: (0, 0, 0)),
            pl.BlockSpec((16, ROWS, COLS * N_MZ), lambda i: (jnp.maximum(i, 1) - 1, 0, 0)),
            pl.BlockSpec((8, 128), lambda i: (0, 0)),
        ),
        compiler_params=pltpu.CompilerParams(vmem_limit_bytes=32 * 2**20),
    )(parts, score)
    return ion_images, formula_images, chaos[0, :CAP]


def solution(mesh):
    in_specs = (P("pix", "mz", None), P(), P(), P(), P())
    out_specs = (P("mz", "pix", None), P("mz", "pix", None), P("mz"))
    return jax.shard_map(body, mesh=mesh, in_specs=in_specs, out_specs=out_specs, check_vma=False)
```

```python
import math

import jax
import jax.numpy as jnp
import ml_dtypes
import numpy as np
from jax import lax
from jax.experimental import pallas as pl
from jax.experimental.pallas import tpu as pltpu
from jax.sharding import PartitionSpec as P

MESH = pl.DeviceIdType.MESH
F32, BF16 = jnp.float32, jnp.bfloat16

CAP = 48
N_MZ, N_PIX = 16, 8
SIDE = 4
ROWS, COLS, BINS = 32, 64, 256
GROUPS = ROWS // 4
PIXELS = ROWS * COLS
EXTRA = 128
TILES = (PIXELS + EXTRA) // 128
PARTS = 4

gauss_raw = [math.exp(-offset * offset / 4.5) for offset in range(-3, 4)]
taps = [value / sum(gauss_raw) for value in gauss_raw]

ORDER = [(0, 1), (1, 0), (0, 3), (3, 0), (1, 1), (3, 3), (1, 3), (3, 1), (2, 0), (0, 2), (2, 1), (1, 2), (2, 3), (3, 2), (2, 2)]


def tap(offset):
    return taps[offset + 3] if -3 <= offset <= 3 else 0.0


def split(matrix):
    high = matrix.astype(ml_dtypes.bfloat16)
    low = (matrix - high.astype(np.float64)).astype(ml_dtypes.bfloat16)
    return high, low


def constants():
    own = np.zeros((256, 256))
    sides = np.zeros((256, 32))
    pick = np.zeros((32, 256))
    for r in range(4):
        for c in range(COLS):
            for k in range(COLS):
                own[r * COLS + c, r * COLS + k] = tap(k - c)
            for j in range(4):
                sides[r * COLS + c, r * 4 + j] = tap(j - 4 - c)
                sides[r * COLS + c, 16 + r * 4 + j] = tap(COLS + j - c)
        for j in range(4):
            pick[r * 4 + j, r * COLS + j] = 1.0
            pick[16 + r * 4 + j, r * COLS + COLS - 4 + j] = 1.0
    seam = np.zeros((64, 320))
    for r in range(ROWS):
        for k in range(ROWS + 8):
            down = tap(k - 4 - r)
            for j in range(4):
                for edge in range(2):
                    seam[edge * 32 + r, k * 4 + j] = down * tap(j - 4 + 1 - edge)
                    seam[edge * 32 + r, 160 + k * 4 + j] = down * tap(j + 1 - edge)
    own_high, own_low = split(own)
    sides_high, sides_low = split(sides)
    blank = np.zeros((256, 64), ml_dtypes.bfloat16)
    first = np.concatenate([own_high, own_low, sides_high, sides_low, blank], axis=1)
    seam_high, seam_low = split(seam)
    second = np.zeros((96, 640), ml_dtypes.bfloat16)
    second[:64] = np.concatenate([seam_high, seam_low], axis=1)
    second[64:, :256] = pick.astype(ml_dtypes.bfloat16)
    return first, second


def dot(a, b):
    return jnp.dot(a, b, preferred_element_type=F32)


def dot_nt(a, b):
    return lax.dot_general(a, b, (((1,), (1,)), ((), ())), preferred_element_type=F32)


def iota(shape, axis):
    return lax.broadcasted_iota(jnp.int32, shape, axis)


def produce_kernel(
    spectra, owner_in, peaks_in, pattern_index_in, patterns_in, blur_in, more_in, parts, score,
    owner, peaks, pattern_index, patterns, blur, more, xs, pack_left, pack_right, left, right, ys, ion, coef, form, out, note, notes, total, totals,
    load_sem, halo_send, halo_recv, part_send, part_recv, part_own, note_send, note_recv, total_send, total_recv,
):
    pix, mz = lax.axis_index("pix"), lax.axis_index("mz")
    z, y = mz // SIDE, mz % SIDE

    def device(dp, dm):
        return {"pix": (pix + dp + N_PIX) % N_PIX, "mz": (mz + dm + N_MZ) % N_MZ}

    def peer(dz, dy):
        return ((z + dz) % SIDE) * SIDE + (y + dy) % SIDE

    def remote(src, dst, send, recv, target):
        return pltpu.make_async_remote_copy(
            src_ref=src, dst_ref=dst, send_sem=send, recv_sem=recv, device_id=target, device_id_type=MESH
        )

    sources = [spectra, more_in, blur_in, owner_in, peaks_in, pattern_index_in, patterns_in]
    targets = [xs.at[pl.ds(1, GROUPS)], more, blur, owner, peaks, pattern_index, patterns]
    loads = [pltpu.make_async_copy(src, dst, load_sem.at[i]) for i, (src, dst) in enumerate(zip(sources, targets))]
    for copy in loads:
        copy.start()

    barrier = pltpu.get_barrier_semaphore()
    near = [(0, 1), (0, -1), (1, 0), (-1, 0), (1, 1), (1, -1), (-1, 1), (-1, -1)]
    for dp, dm in near[2:]:
        pl.semaphore_signal(barrier, inc=1, device_id=device(dp, dm), device_id_type=MESH)
    for dz, dy in ORDER:
        pl.semaphore_signal(barrier, inc=1, device_id={"mz": peer(dz, dy)}, device_id_type=MESH)
    for dp in range(2, N_PIX - 1):
        pl.semaphore_signal(barrier, inc=1, device_id=device(dp, 0), device_id_type=MESH)

    for copy in loads:
        copy.wait()
    pick = more[64:96, 0:256]

    def pack(g, carry):
        ends = dot(pick, xs[g]).astype(BF16)
        pack_left[g] = ends[0:16]
        pack_right[g] = ends[16:32]
        return carry

    lax.fori_loop(1, GROUPS + 1, pack, 0)
    pl.semaphore_wait(barrier, 6 + len(ORDER) + N_PIX - 3)

    inner = pl.ds(1, GROUPS)
    halo = [
        (xs.at[GROUPS], xs.at[0], (1, 0)),
        (xs.at[1], xs.at[GROUPS + 1], (-1, 0)),
        (pack_right.at[inner], left.at[inner], (0, 1)),
        (pack_left.at[inner], right.at[inner], (0, -1)),
        (pack_right.at[GROUPS], left.at[0], (1, 1)),
        (pack_right.at[1], left.at[GROUPS + 1], (-1, 1)),
        (pack_left.at[GROUPS], right.at[0], (1, -1)),
        (pack_left.at[1], right.at[GROUPS + 1], (-1, -1)),
    ]
    halo = [
        remote(src, dst, halo_send.at[i], halo_recv.at[i], device(*to)) for i, (src, dst, to) in enumerate(halo)
    ]
    for copy in halo:
        copy.start()

    blur_high, blur_low, blur_sides = blur[:, 0:256], blur[:, 256:512], blur[:, 512:576]

    def columns_own(g, carry):
        x = xs[g]
        ys[g] = dot(blur_high, x) + dot(blur_low, x)
        return carry

    lax.fori_loop(1, GROUPS + 1, columns_own, 0)

    count = owner.shape[0]
    owner_row = owner[...].reshape(1, count)
    owner_hot = (iota((N_MZ, count), 0) == owner_row).astype(F32)
    before = (iota((count, count), 0) < iota((count, count), 1)).astype(F32).astype(BF16)
    earlier = dot(owner_hot.astype(BF16), before)
    rank = jnp.sum(earlier * owner_hot, axis=0, keepdims=True)
    slot = owner_row * CAP + rank.astype(jnp.int32)
    pattern_hot = (iota((patterns.shape[1], count), 0) == pattern_index[...].reshape(1, count)).astype(F32).astype(BF16)
    weight = dot(patterns[...].astype(BF16), pattern_hot)
    spread = jnp.zeros((BINS, count), F32)
    for k in range(peaks.shape[0]):
        spread += jnp.where(iota((BINS, count), 0) == peaks[k : k + 1, :], weight[k : k + 1, :], 0.0)
    spread = spread.astype(BF16)
    place = iota((256, count), 0)
    place = (place // 16) * CAP + place % 16
    coef[0] = (iota((256, BINS), 0) == iota((256, BINS), 1)).astype(F32).astype(BF16)
    for q in range(1, PARTS):
        slot_hot = (place + (q - 1) * 16 == slot).astype(F32).astype(BF16)
        coef[q] = dot_nt(slot_hot, spread).astype(BF16)

    for copy in halo:
        copy.wait()

    @pl.when(pix == 0)
    def _():
        xs[0] = jnp.zeros(xs.shape[1:], BF16)
        left[0] = jnp.zeros(left.shape[1:], BF16)
        right[0] = jnp.zeros(right.shape[1:], BF16)

    @pl.when(pix == N_PIX - 1)
    def _():
        xs[GROUPS + 1] = jnp.zeros(xs.shape[1:], BF16)
        left[GROUPS + 1] = jnp.zeros(left.shape[1:], BF16)
        right[GROUPS + 1] = jnp.zeros(right.shape[1:], BF16)

    @pl.when(mz == 0)
    def _():
        left[...] = jnp.zeros(left.shape, BF16)

    @pl.when(mz == N_MZ - 1)
    def _():
        right[...] = jnp.zeros(right.shape, BF16)

    columns_own(0, 0)
    columns_own(GROUPS + 1, 0)

    def columns_sides(g, carry):
        sides = jnp.concatenate([left[g], right[g], left[g], right[g]], axis=0)
        ys[g] += dot(blur_sides, sides)
        return carry

    lax.fori_loop(0, GROUPS + 2, columns_sides, 0)

    for g in (0, GROUPS + 1):
        pack_left[g] = dot(pick[0:16], xs[g]).astype(BF16)
    edge = jnp.concatenate([left[...].reshape(160, BINS), pack_left[...].reshape(160, BINS)], axis=0)
    ion[PIXELS + 64 : PIXELS + 128] = (dot(more[0:64, 0:320], edge) + dot(more[0:64, 320:640], edge)).astype(BF16)

    def row(k, first):
        result = taps[3] * first(k + 3)
        for i in range(3):
            result = result + taps[i] * (first(k + i) + first(k + 6 - i))
        return result

    def slab(k):
        return ys[k // 4, pl.ds(pl.multiple_of((k % 4) * COLS, COLS), COLS), :]

    def rows(r, carry):
        at = pl.multiple_of((r % 16) * 128 + (r // 16) * 64, 64)
        ion[pl.ds(at, COLS), :] = row(r + 1, slab).astype(BF16)
        return carry

    lax.fori_loop(0, ROWS, rows, 0)
    ion[PIXELS : PIXELS + 64] = row(0, slab).astype(BF16)

    def product(q):
        def tile(n, carry):
            at = pl.multiple_of(n * 256, 256)
            result = dot_nt(coef[q], ion[pl.ds(at, 256), :])
            form[q, pl.ds(pl.multiple_of(n * 512, 512), 256), :] = result[:, 0:128]
            form[q, pl.ds(pl.multiple_of(n * 512 + 256, 256), 256), :] = result[:, 128:256]
            return carry

        lax.fori_loop(0, PIXELS // 256, tile, 0)
        form[q, pl.ds(PIXELS * 2, 256), :] = dot_nt(coef[q], ion[pl.ds(PIXELS, 128), :])

        def turn(d, carry):
            for s in range(16):
                out[q, d, s] = form[q, pl.ds(d * 16 + s, 16, stride=256), :].astype(BF16)
            return carry

        lax.fori_loop(0, N_MZ, turn, 0)

    def send(q):
        copies = []
        for i, (dz, dy) in enumerate(ORDER):
            to = peer(dz, dy)
            copies.append(
                remote(out.at[q, to], parts.at[q, mz], part_send.at[q, i], part_recv.at[q, i], {"mz": to})
            )
        copies.append(pltpu.make_async_copy(out.at[q, mz], parts.at[q, mz], part_own.at[q]))
        for copy in copies:
            copy.start()
        return copies

    product(0)
    copies = send(0)
    product(1)
    copies += send(1)
    product(2)
    product(3)

    lane, sub = iota((8, 128), 1), iota((8, 128), 0)
    keep_across = (lane % 64 != 0).astype(F32)
    keep_seam = jnp.where(mz > 0, (lane >= 96).astype(F32), 0.0)
    keep_top = jnp.where(pix > 0, 1.0, jnp.where(lane < 64, 0.0, 1.0))
    note[...] = jnp.zeros(note.shape, F32)

    for q in range(1, PARTS):
        def scores(d, carry, q=q):
            acc = jnp.zeros((8, 128), F32)
            for half in range(2):
                def value(j):
                    at = pl.multiple_of(j * 256 + d * 16 + half * 8, 8)
                    return form[q, pl.ds(at, 8), :].astype(BF16).astype(F32)

                extra = value(TILES - 1)
                prior = jnp.where(lane < 64, extra, pltpu.roll(value(15), 64, 1))
                across = jnp.zeros((8, 128), F32)
                down = jnp.zeros((8, 128), F32)
                energy = jnp.zeros((8, 128), F32)
                for j in range(16):
                    now = value(j)
                    step = now - pltpu.roll(now, 1, 1)
                    across += step * step
                    step = now - prior
                    if j == 0:
                        step = step * keep_top
                    down += step * step
                    energy += now * now
                    prior = now
                step = extra - pltpu.roll(extra, 32, 1)
                rough = across * keep_across + down + step * step * keep_seam
                rough = jnp.sum(rough, axis=1, keepdims=True)
                energy = jnp.sum(energy, axis=1, keepdims=True)
                base = (q - 1) * 16 + half * 8
                acc += jnp.where(lane == sub + base, rough, 0.0) + jnp.where(lane == sub + base + 64, energy, 0.0)
            note[d] += acc
            return carry

        lax.fori_loop(0, N_MZ, scores, 0)

    small = []
    for i, (dz, dy) in enumerate(ORDER):
        to = peer(dz, dy)
        small.append(remote(note.at[to], notes.at[mz], note_send.at[i], note_recv.at[i], {"mz": to}))
    for copy in small:
        copy.start()
    copies += send(2)
    for copy in small:
        copy.wait()
    notes[mz] = note[mz]
    total[...] = jnp.sum(notes[...], axis=0)
    small = []
    for dp in range(1, N_PIX):
        to = device(dp, 0)
        small.append(remote(total, totals.at[pix], total_send.at[dp], total_recv.at[dp], to))
    for copy in small:
        copy.start()
    copies += send(3)
    for copy in small:
        copy.wait()
    totals[pix] = total[...]
    final = jnp.sum(jnp.sum(totals[...], axis=0), axis=0, keepdims=True)
    final = final / (pltpu.roll(final, 64, 1) + 1e-5)
    score[...] = jnp.broadcast_to(final, (8, 128))
    for copy in copies:
        copy.wait()


def place_kernel(parts, score, ion_out, form_out, chaos_out):
    step = pl.program_id(0)

    def fill(target):
        for j in range(N_MZ // 2):
            a, b = parts[step, 2 * j], parts[step, 2 * j + 1]
            at = slice(j * 128, (j + 1) * 128)
            target[:, 0:16, at] = jnp.concatenate([a[:, :, :64], b[:, :, :64]], axis=2)
            target[:, 16:32, at] = jnp.concatenate([a[:, :, 64:], b[:, :, 64:]], axis=2)

    @pl.when(step == 0)
    def _():
        fill(ion_out)
        chaos_out[...] = score[...]

    @pl.when(step > 0)
    def _():
        fill(form_out)


def body(spectra, owner, peaks, pattern_index, patterns):
    first, second = constants()
    dma = pltpu.SemaphoreType.DMA
    peers = len(ORDER)
    parts, score = pl.pallas_call(
        produce_kernel,
        out_shape=(
            jax.ShapeDtypeStruct((PARTS, N_MZ, 16, 16, 128), BF16),
            jax.ShapeDtypeStruct((8, 128), F32),
        ),
        in_specs=[pl.BlockSpec(memory_space=pltpu.HBM)] * 7,
        out_specs=(pl.BlockSpec(memory_space=pl.ANY), pl.BlockSpec(memory_space=pltpu.VMEM)),
        scratch_shapes=[
            pltpu.VMEM(owner.shape, jnp.int32),
            pltpu.VMEM(peaks.shape[::-1], jnp.int32),
            pltpu.VMEM(pattern_index.shape, jnp.int32),
            pltpu.VMEM(patterns.shape[::-1], F32),
            pltpu.VMEM(first.shape, BF16),
            pltpu.VMEM(second.shape, BF16),
            pltpu.VMEM((GROUPS + 2, 256, BINS), BF16),
            pltpu.VMEM((GROUPS + 2, 16, BINS), BF16),
            pltpu.VMEM((GROUPS + 2, 16, BINS), BF16),
            pltpu.VMEM((GROUPS + 2, 16, BINS), BF16),
            pltpu.VMEM((GROUPS + 2, 16, BINS), BF16),
            pltpu.VMEM((GROUPS + 2, 256, BINS), F32),
            pltpu.VMEM((PIXELS + EXTRA, BINS), BF16),
            pltpu.VMEM((PARTS, 256, BINS), BF16),
            pltpu.VMEM((PARTS, TILES * 256, 128), F32),
            pltpu.VMEM((PARTS, N_MZ, 16, 16, 128), BF16),
            pltpu.VMEM((N_MZ, 8, 128), F32),
            pltpu.VMEM((N_MZ, 8, 128), F32),
            pltpu.VMEM((8, 128), F32),
            pltpu.VMEM((N_PIX, 8, 128), F32),
            dma((7,)),
            dma((8,)),
            dma((8,)),
            dma((PARTS, peers)),
            dma((PARTS, peers)),
            dma((PARTS,)),
            dma((peers,)),
            dma((peers,)),
            dma((N_PIX,)),
            dma((N_PIX,)),
        ],
        compiler_params=pltpu.CompilerParams(
            collective_id=0, has_side_effects=True, vmem_limit_bytes=48 * 2**20
        ),
    )(
        *[pltpu.with_memory_space_constraint(x, pltpu.HBM) for x in (spectra.reshape(GROUPS, 256, BINS),
        owner,
        peaks.T,
        pattern_index,
        patterns.T,
        jnp.asarray(first),
        jnp.asarray(second))]
    )
    ion_images, formula_images, chaos = pl.pallas_call(
        place_kernel,
        grid=(PARTS,),
        out_shape=(
            jax.ShapeDtypeStruct((16, ROWS, COLS * N_MZ), BF16),
            jax.ShapeDtypeStruct((CAP, ROWS, COLS * N_MZ), BF16),
            jax.ShapeDtypeStruct((8, 128), F32),
        ),
        in_specs=[
            pl.BlockSpec(memory_space=pltpu.VMEM),
            pl.BlockSpec(memory_space=pltpu.VMEM),
        ],
        out_specs=(
            pl.BlockSpec((16, ROWS, COLS * N_MZ), lambda i: (0, 0, 0)),
            pl.BlockSpec((16, ROWS, COLS * N_MZ), lambda i: (jnp.maximum(i, 1) - 1, 0, 0)),
            pl.BlockSpec((8, 128), lambda i: (0, 0)),
        ),
        compiler_params=pltpu.CompilerParams(vmem_limit_bytes=32 * 2**20),
    )(parts, score)
    return ion_images, formula_images, chaos[0, :CAP]


def solution(mesh):
    in_specs = (P("pix", "mz", None), P(), P(), P(), P())
    out_specs = (P("mz", "pix", None), P("mz", "pix", None), P("mz"))
    return jax.shard_map(body, mesh=mesh, in_specs=in_specs, out_specs=out_specs, check_vma=False)
```

```python
import math

import jax
import jax.numpy as jnp
import ml_dtypes
import numpy as np
from jax import lax
from jax.experimental import pallas as pl
from jax.experimental.pallas import tpu as pltpu
from jax.sharding import PartitionSpec as P

MESH = pl.DeviceIdType.MESH
F32, BF16 = jnp.float32, jnp.bfloat16

CAP = 48
N_MZ, N_PIX = 16, 8
SIDE = 4
ROWS, COLS, BINS = 32, 64, 256
GROUPS = ROWS // 4
PIXELS = ROWS * COLS
EXTRA = 128
PARTS = 4

gauss_raw = [math.exp(-offset * offset / 4.5) for offset in range(-3, 4)]
taps = [value / sum(gauss_raw) for value in gauss_raw]

ORDER = [(0, 1), (1, 0), (0, 3), (3, 0), (1, 1), (3, 3), (1, 3), (3, 1), (2, 0), (0, 2), (2, 1), (1, 2), (2, 3), (3, 2), (2, 2)]


def tap(offset):
    return taps[offset + 3] if -3 <= offset <= 3 else 0.0


def split(matrix):
    high = matrix.astype(ml_dtypes.bfloat16)
    low = (matrix - high.astype(np.float64)).astype(ml_dtypes.bfloat16)
    return high, low


def constants():
    own = np.zeros((256, 256))
    sides = np.zeros((256, 32))
    pick = np.zeros((32, 256))
    for r in range(4):
        for c in range(COLS):
            for k in range(COLS):
                own[r * COLS + c, r * COLS + k] = tap(k - c)
            for j in range(4):
                sides[r * COLS + c, r * 4 + j] = tap(j - 4 - c)
                sides[r * COLS + c, 16 + r * 4 + j] = tap(COLS + j - c)
        for j in range(4):
            pick[r * 4 + j, r * COLS + j] = 1.0
            pick[16 + r * 4 + j, r * COLS + COLS - 4 + j] = 1.0
    seam = np.zeros((64, 320))
    for r in range(ROWS):
        for k in range(ROWS + 8):
            down = tap(k - 4 - r)
            for j in range(4):
                for edge in range(2):
                    seam[edge * 32 + r, k * 4 + j] = down * tap(j - 4 + 1 - edge)
                    seam[edge * 32 + r, 160 + k * 4 + j] = down * tap(j + 1 - edge)
    own_high, own_low = split(own)
    sides_high, sides_low = split(sides)
    blank = np.zeros((256, 64), ml_dtypes.bfloat16)
    first = np.concatenate([own_high, own_low, sides_high, sides_low, blank], axis=1)
    seam_high, seam_low = split(seam)
    second = np.zeros((96, 640), ml_dtypes.bfloat16)
    second[:64] = np.concatenate([seam_high, seam_low], axis=1)
    second[64:, :256] = pick.astype(ml_dtypes.bfloat16)
    wide = np.zeros((512, 256))
    for strip in range(4):
        for half in range(2):
            for c in range(COLS):
                for k in range(128):
                    wide[strip * 128 + half * COLS + c, half * 128 + k] = tap((strip - 1) * COLS + c - k)
    return first, second, np.concatenate(split(wide), axis=1)


def dot(a, b):
    return jnp.dot(a, b, preferred_element_type=F32)


def dot_nt(a, b):
    return lax.dot_general(a, b, (((1,), (1,)), ((), ())), preferred_element_type=F32)


def iota(shape, axis):
    return lax.broadcasted_iota(jnp.int32, shape, axis)


def rolled_tiles(tiles):
    return jnp.swapaxes(jnp.stack(tiles), 0, 1)


def join_strips(part, target):
    for j in range(N_MZ // 2):
        a, b = part[2 * j], part[2 * j + 1]
        at = slice(j * 128, (j + 1) * 128)
        target[:, 0:16, at] = jnp.concatenate([a[:, :, :64], b[:, :, :64]], axis=2)
        target[:, 16:32, at] = jnp.concatenate([a[:, :, 64:], b[:, :, 64:]], axis=2)


def produce_kernel(
    spectra, owner_in, peaks_in, pattern_index_in, patterns_in, blur_in, more_in, wide_in, done, last, score,
    owner, peaks, pattern_index, patterns, blur, more, wide, xs, pack_left, pack_right, left, right, ys, ion, coef,
    form, out, raw, land, rows_wide, joined, note, notes, total, totals,
    load_sem, halo_send, halo_recv, part_send, part_recv, part_own, rows_send, rows_recv, done_sem,
    note_send, note_recv, total_send, total_recv,
):
    pix, mz = lax.axis_index("pix"), lax.axis_index("mz")
    z, y = mz // SIDE, mz % SIDE

    def device(dp, dm):
        return {"pix": (pix + dp + N_PIX) % N_PIX, "mz": (mz + dm + N_MZ) % N_MZ}

    def peer(dz, dy):
        return ((z + dz) % SIDE) * SIDE + (y + dy) % SIDE

    def remote(src, dst, send, recv, target):
        return pltpu.make_async_remote_copy(
            src_ref=src, dst_ref=dst, send_sem=send, recv_sem=recv, device_id=target, device_id_type=MESH
        )

    sources = [spectra, more_in, blur_in, owner_in, peaks_in, pattern_index_in, patterns_in, wide_in]
    targets = [xs.at[pl.ds(1, GROUPS)], more, blur, owner, peaks, pattern_index, patterns, wide]
    loads = [pltpu.make_async_copy(src, dst, load_sem.at[i]) for i, (src, dst) in enumerate(zip(sources, targets))]
    for copy in loads:
        copy.start()

    barrier = pltpu.get_barrier_semaphore()
    near = [(1, 0), (-1, 0), (1, 1), (1, -1), (-1, 1), (-1, -1)]
    for dz, dy in ORDER:
        pl.semaphore_signal(barrier, inc=1, device_id={"mz": peer(dz, dy)}, device_id_type=MESH)
    for dp, dm in near:
        pl.semaphore_signal(barrier, inc=1, device_id=device(dp, dm), device_id_type=MESH)
    for dp in range(2, N_PIX - 1):
        pl.semaphore_signal(barrier, inc=1, device_id=device(dp, 0), device_id_type=MESH)

    for copy in loads[:2]:
        copy.wait()
    pick = more[64:96, 0:256]
    for g in range(1, GROUPS + 1):
        ends = dot(pick, xs[g]).astype(BF16)
        pack_left[g] = ends[0:16]
        pack_right[g] = ends[16:32]
    same = (iota((BINS, BINS), 0) == iota((BINS, BINS), 1)).astype(F32).astype(BF16)
    tiles = []
    for n in range(8):
        rows_here = [xs[1 + r // 4, (r % 4) * COLS : (r % 4 + 1) * COLS, :] for r in (2 * n, 2 * n + 16, 2 * n + 1, 2 * n + 17)]
        turned = dot_nt(same, jnp.concatenate(rows_here, axis=0)).astype(BF16)
        tiles += [turned[:, 0:128], turned[:, 128:256]]
    for d in range(N_MZ):
        out[0, d] = rolled_tiles([tile[d * 16 : (d + 1) * 16] for tile in tiles])

    pl.semaphore_wait(barrier, len(ORDER) + len(near) + N_PIX - 3)

    inner = pl.ds(1, GROUPS)
    halo = [
        (xs.at[GROUPS], xs.at[0], (1, 0)),
        (xs.at[1], xs.at[GROUPS + 1], (-1, 0)),
        (pack_right.at[inner], left.at[inner], (0, 1)),
        (pack_left.at[inner], right.at[inner], (0, -1)),
        (pack_right.at[GROUPS], left.at[0], (1, 1)),
        (pack_right.at[1], left.at[GROUPS + 1], (-1, 1)),
        (pack_left.at[GROUPS], right.at[0], (1, -1)),
        (pack_left.at[1], right.at[GROUPS + 1], (-1, -1)),
    ]
    halo = [
        remote(src, dst, halo_send.at[i], halo_recv.at[i], device(*to)) for i, (src, dst, to) in enumerate(halo)
    ]
    for copy in halo:
        copy.start()

    def send(q, target):
        copies = []
        for i, (dz, dy) in enumerate(ORDER):
            to = peer(dz, dy)
            copies.append(remote(out.at[q, to], target.at[mz], part_send.at[q, i], part_recv.at[q, i], {"mz": to}))
        copies.append(pltpu.make_async_copy(out.at[q, mz], target.at[mz], part_own.at[q]))
        for copy in copies:
            copy.start()
        return copies

    sent_raw = send(0, raw)

    loads[2].wait()
    blur_high, blur_low, blur_sides = blur[:, 0:256], blur[:, 256:512], blur[:, 512:576]

    def columns_own(g):
        ys[g] = dot(blur_high, xs[g]) + dot(blur_low, xs[g])

    for g in range(1, GROUPS + 1):
        columns_own(g)

    for copy in loads[3:]:
        copy.wait()
    count = owner.shape[0]
    owner_row = owner[...].reshape(1, count)
    owner_hot = (iota((N_MZ, count), 0) == owner_row).astype(F32)
    before = (iota((count, count), 0) < iota((count, count), 1)).astype(F32).astype(BF16)
    earlier = dot(owner_hot.astype(BF16), before)
    rank = jnp.sum(earlier * owner_hot, axis=0, keepdims=True)
    slot = owner_row * CAP + rank.astype(jnp.int32)
    pattern_hot = (iota((patterns.shape[1], count), 0) == pattern_index[...].reshape(1, count)).astype(F32).astype(BF16)
    weight = dot(patterns[...].astype(BF16), pattern_hot)
    spread = jnp.zeros((BINS, count), F32)
    for k in range(peaks.shape[0]):
        spread += jnp.where(iota((BINS, count), 0) == peaks[k : k + 1, :], weight[k : k + 1, :], 0.0)
    spread = spread.astype(BF16)
    place = iota((256, count), 0)
    place = (place // 16) * CAP + place % 16
    for q in range(1, PARTS):
        slot_hot = (place + (q - 1) * 16 == slot).astype(F32).astype(BF16)
        coef[q - 1] = dot_nt(slot_hot, spread).astype(BF16)

    for copy in halo:
        copy.wait()

    @pl.when(pix == 0)
    def _():
        xs[0] = jnp.zeros(xs.shape[1:], BF16)
        left[0] = jnp.zeros(left.shape[1:], BF16)
        right[0] = jnp.zeros(right.shape[1:], BF16)

    @pl.when(pix == N_PIX - 1)
    def _():
        xs[GROUPS + 1] = jnp.zeros(xs.shape[1:], BF16)
        left[GROUPS + 1] = jnp.zeros(left.shape[1:], BF16)
        right[GROUPS + 1] = jnp.zeros(right.shape[1:], BF16)

    @pl.when(mz == 0)
    def _():
        left[...] = jnp.zeros(left.shape, BF16)

    @pl.when(mz == N_MZ - 1)
    def _():
        right[...] = jnp.zeros(right.shape, BF16)

    columns_own(0)
    columns_own(GROUPS + 1)
    for g in range(GROUPS + 2):
        sides = jnp.concatenate([left[g], right[g], left[g], right[g]], axis=0)
        ys[g] += dot(blur_sides, sides)

    for g in (0, GROUPS + 1):
        pack_left[g] = dot(pick[0:16], xs[g]).astype(BF16)
    edge = jnp.concatenate([left[...].reshape(160, BINS), pack_left[...].reshape(160, BINS)], axis=0)
    ion[PIXELS + 64 : PIXELS + 128] = (dot(more[0:64, 0:320], edge) + dot(more[0:64, 320:640], edge)).astype(BF16)

    def rows(c, carry):
        for lanes in (slice(0, 128), slice(128, 256)):
            lines = [ys[k // 4, pl.ds(pl.multiple_of((k % 4) * COLS + c * 16, 16), 16), lanes] for k in range(ROWS + 7)]
            for r in range(-1, ROWS):
                result = taps[3] * lines[r + 4]
                for i in range(3):
                    result = result + taps[i] * (lines[r + 1 + i] + lines[r + 7 - i])
                at = PIXELS if r < 0 else (r % 16) * 128 + (r // 16) * 64
                ion[pl.ds(pl.multiple_of(at + c * 16, 16), 16), lanes] = result.astype(BF16)
        return carry

    lax.fori_loop(0, COLS // 16, rows, 0)

    def product(q):
        tiles = []
        for n in range(PIXELS // 256):
            result = dot_nt(coef[q - 1], ion[n * 256 : (n + 1) * 256, :]).astype(BF16)
            tiles += [result[:, 0:128], result[:, 128:256]]
        for j, tile in enumerate(tiles):
            form[q - 1, j] = tile
        form[q - 1, 16] = dot_nt(coef[q - 1], ion[PIXELS : PIXELS + 128, :]).astype(BF16)
        for d in range(N_MZ):
            out[q, d] = rolled_tiles([tile[d * 16 : (d + 1) * 16] for tile in tiles])

    product(1)
    sent_1 = send(1, land.at[0])
    product(2)
    product(3)

    lane, sub = iota((64, 128), 1), iota((8, 128), 0)
    keep_across = (lane % 64 != 0).astype(F32)
    keep_seam = jnp.where(mz > 0, (lane >= 96).astype(F32), 0.0)
    keep_top = jnp.where(pix > 0, 1.0, jnp.where(lane < 64, 0.0, 1.0))
    note[...] = jnp.zeros(note.shape, F32)

    for q in range(1, PARTS):
        def scores(d, carry, q=q):
            def value(j):
                return form[q - 1, j, pl.ds(pl.multiple_of(d * 64, 64), 64), :].astype(F32)

            extra = value(16)
            prior = jnp.where(lane < 64, extra, pltpu.roll(value(15), 64, 1))
            across = jnp.zeros((64, 128), F32)
            down = jnp.zeros((64, 128), F32)
            energy = jnp.zeros((64, 128), F32)
            for j in range(16):
                now = value(j)
                step = now - pltpu.roll(now, 1, 1)
                across += step * step
                step = now - prior
                if j == 0:
                    step = step * keep_top
                down += step * step
                energy += now * now
                prior = now
            step = extra - pltpu.roll(extra, 32, 1)
            rough = across * keep_across + down + step * step * keep_seam
            rough = jnp.sum(rough, axis=1, keepdims=True)
            energy = jnp.sum(energy, axis=1, keepdims=True)
            for k in range(4):
                acc = jnp.zeros((8, 128), F32)
                for half in range(2):
                    at = k * 16 + half * 8
                    base = sub + ((q - 1) * 16 + half * 8)
                    acc += jnp.where(lane[0:8] == base, rough[at : at + 8], 0.0)
                    acc += jnp.where(lane[0:8] == base + 64, energy[at : at + 8], 0.0)
                note[d * 4 + k] += acc
            return carry

        lax.fori_loop(0, N_MZ // 4, scores, 0)

    small = []
    for i, (dz, dy) in enumerate(ORDER):
        to = peer(dz, dy)
        small.append(remote(note.at[to], notes.at[mz], note_send.at[i], note_recv.at[i], {"mz": to}))
    for copy in small:
        copy.start()
    sent_2 = send(2, land.at[1])

    for copy in sent_raw:
        copy.wait()
    blank = jnp.zeros((256, 128), BF16)
    for j in range(N_MZ // 2):
        strips = [raw[k].reshape(256, 128) if 0 <= k < N_MZ else blank for k in range(2 * j - 1, 2 * j + 3)]
        strips = jnp.concatenate(strips, axis=1)
        result = (dot(strips, wide[:, 0:256]) + dot(strips, wide[:, 256:512])).reshape(16, 16, 256)
        rows_wide[:, 8:24, j * 128 : (j + 1) * 128] = result[:, :, 0:128]
        rows_wide[:, 24:40, j * 128 : (j + 1) * 128] = result[:, :, 128:256]
    above, below = pl.ds(0, 8), pl.ds(40, 8)
    edges = [
        remote(rows_wide.at[:, pl.ds(32, 8)], rows_wide.at[:, above], rows_send.at[0], rows_recv.at[0], device(1, 0)),
        remote(rows_wide.at[:, pl.ds(8, 8)], rows_wide.at[:, below], rows_send.at[1], rows_recv.at[1], device(-1, 0)),
    ]
    for copy in edges:
        copy.start()

    for copy in small:
        copy.wait()
    notes[mz] = note[mz]
    total[...] = jnp.sum(notes[...], axis=0)
    small = []
    for dp in range(1, N_PIX):
        to = device(dp, 0)
        small.append(remote(total, totals.at[pix], total_send.at[dp], total_recv.at[dp], to))
    for copy in small:
        copy.start()
    sent_3 = send(3, last)

    for copy in edges:
        copy.wait()

    @pl.when(pix == 0)
    def _():
        rows_wide[:, above, :] = jnp.zeros((16, 8, COLS * N_MZ), F32)

    @pl.when(pix == N_PIX - 1)
    def _():
        rows_wide[:, below, :] = jnp.zeros((16, 8, COLS * N_MZ), F32)

    def own_rows(b, carry):
        for j in range(N_MZ // 2):
            x = rows_wide[b, :, j * 128 : (j + 1) * 128]
            result = taps[3] * x[8:40]
            for i in range(3):
                result = result + taps[i] * (x[5 + i : 37 + i] + x[11 - i : 43 - i])
            joined[b, :, j * 128 : (j + 1) * 128] = result.astype(BF16)
        return carry

    lax.fori_loop(0, 16, own_rows, 0)
    stores = [pltpu.make_async_copy(joined.at[pl.ds(0, 16)], done.at[pl.ds(0, 16)], done_sem.at[0])]
    stores[0].start()

    for copy in small:
        copy.wait()
    totals[pix] = total[...]
    final = jnp.sum(jnp.sum(totals[...], axis=0), axis=0, keepdims=True)
    final = final / (pltpu.roll(final, 64, 1) + 1e-5)
    score[...] = jnp.broadcast_to(final, (8, 128))

    for q, copies in ((1, sent_1), (2, sent_2)):
        for copy in copies:
            copy.wait()
        at = pl.ds(q * 16, 16)
        join_strips(land.at[q - 1], joined.at[at])
        stores.append(pltpu.make_async_copy(joined.at[at], done.at[at], done_sem.at[q]))
        stores[q].start()
    for copy in stores + sent_3:
        copy.wait()


def place_kernel(done, last, score, ion_out, form_out, chaos_out, joined, sems):
    copies = [
        pltpu.make_async_copy(done.at[pl.ds(0, 16)], ion_out, sems.at[0]),
        pltpu.make_async_copy(done.at[pl.ds(16, 32)], form_out.at[pl.ds(0, 32)], sems.at[1]),
        pltpu.make_async_copy(joined, form_out.at[pl.ds(32, 16)], sems.at[2]),
    ]
    copies[0].start()
    copies[1].start()
    join_strips(last, joined)
    copies[2].start()
    chaos_out[...] = score[...]
    for copy in copies:
        copy.wait()


def body(spectra, owner, peaks, pattern_index, patterns):
    first, second, third = constants()
    dma = pltpu.SemaphoreType.DMA
    vmem, hbm, free = (pl.BlockSpec(memory_space=space) for space in (pltpu.VMEM, pltpu.HBM, pl.ANY))
    peers = len(ORDER)
    wide_cols = COLS * N_MZ
    inputs = (
        spectra.reshape(GROUPS, 256, BINS), owner, peaks.T, pattern_index, patterns.T,
        jnp.asarray(first), jnp.asarray(second), jnp.asarray(third),
    )
    inputs = [pltpu.with_memory_space_constraint(x, pltpu.HBM) for x in inputs]
    done, last, score = pl.pallas_call(
        produce_kernel,
        out_shape=(
            jax.ShapeDtypeStruct((48, ROWS, wide_cols), BF16),
            jax.ShapeDtypeStruct((N_MZ, 16, 16, 128), BF16),
            jax.ShapeDtypeStruct((8, 128), F32),
        ),
        in_specs=[hbm] * len(inputs),
        out_specs=(free, free, vmem),
        scratch_shapes=[pltpu.VMEM(x.shape, x.dtype) for x in inputs[1:]]
        + [
            pltpu.VMEM((GROUPS + 2, 256, BINS), BF16),
            pltpu.VMEM((GROUPS + 2, 16, BINS), BF16),
            pltpu.VMEM((GROUPS + 2, 16, BINS), BF16),
            pltpu.VMEM((GROUPS + 2, 16, BINS), BF16),
            pltpu.VMEM((GROUPS + 2, 16, BINS), BF16),
            pltpu.VMEM((GROUPS + 2, 256, BINS), F32),
            pltpu.VMEM((PIXELS + EXTRA, BINS), BF16),
            pltpu.VMEM((PARTS - 1, 256, BINS), BF16),
            pltpu.VMEM((PARTS - 1, 17, 256, 128), BF16),
            pltpu.VMEM((PARTS, N_MZ, 16, 16, 128), BF16),
            pltpu.VMEM((N_MZ, 16, 16, 128), BF16),
            pltpu.VMEM((2, N_MZ, 16, 16, 128), BF16),
            pltpu.VMEM((16, ROWS + 16, wide_cols), F32),
            pltpu.VMEM((48, ROWS, wide_cols), BF16),
            pltpu.VMEM((N_MZ, 8, 128), F32),
            pltpu.VMEM((N_MZ, 8, 128), F32),
            pltpu.VMEM((8, 128), F32),
            pltpu.VMEM((N_PIX, 8, 128), F32),
            dma((len(inputs),)),
            dma((8,)),
            dma((8,)),
            dma((PARTS, peers)),
            dma((PARTS, peers)),
            dma((PARTS,)),
            dma((2,)),
            dma((2,)),
            dma((3,)),
            dma((peers,)),
            dma((peers,)),
            dma((N_PIX,)),
            dma((N_PIX,)),
        ],
        compiler_params=pltpu.CompilerParams(
            collective_id=0, has_side_effects=True, vmem_limit_bytes=48 * 2**20
        ),
    )(*inputs)
    ion_images, formula_images, chaos = pl.pallas_call(
        place_kernel,
        out_shape=(
            jax.ShapeDtypeStruct((16, ROWS, wide_cols), BF16),
            jax.ShapeDtypeStruct((CAP, ROWS, wide_cols), BF16),
            jax.ShapeDtypeStruct((8, 128), F32),
        ),
        in_specs=[vmem, vmem, vmem],
        out_specs=(free, free, vmem),
        scratch_shapes=[pltpu.VMEM((16, ROWS, wide_cols), BF16), dma((3,))],
        compiler_params=pltpu.CompilerParams(vmem_limit_bytes=32 * 2**20),
    )(done, last, score)
    return ion_images, formula_images, chaos[0, :CAP]


def solution(mesh):
    in_specs = (P("pix", "mz", None), P(), P(), P(), P())
    out_specs = (P("mz", "pix", None), P("mz", "pix", None), P("mz"))
    return jax.shard_map(body, mesh=mesh, in_specs=in_specs, out_specs=out_specs, check_vma=False)
```

```python
import math

import jax
import jax.numpy as jnp
import ml_dtypes
import numpy as np
from jax import lax
from jax.experimental import pallas as pl
from jax.experimental.pallas import tpu as pltpu
from jax.sharding import PartitionSpec as P

MESH = pl.DeviceIdType.MESH
F32, BF16 = jnp.float32, jnp.bfloat16

CAP = 48
N_MZ, N_PIX = 16, 8
SIDE = 4
ROWS, COLS, BINS = 32, 64, 256
GROUPS = ROWS // 4
PIXELS = ROWS * COLS
EXTRA = 128
PARTS = 4
TURNED = (0, 0, 0, 0)

gauss_raw = [math.exp(-offset * offset / 4.5) for offset in range(-3, 4)]
taps = [value / sum(gauss_raw) for value in gauss_raw]

ORDER = [(0, 1), (1, 0), (0, 3), (3, 0), (1, 1), (3, 3), (1, 3), (3, 1), (2, 0), (0, 2), (2, 1), (1, 2), (2, 3), (3, 2), (2, 2)]


def tap(offset):
    return taps[offset + 3] if -3 <= offset <= 3 else 0.0


def split(matrix):
    high = matrix.astype(ml_dtypes.bfloat16)
    low = (matrix - high.astype(np.float64)).astype(ml_dtypes.bfloat16)
    return high, low


def constants():
    own = np.zeros((256, 256))
    sides = np.zeros((256, 32))
    pick = np.zeros((32, 256))
    for r in range(4):
        for c in range(COLS):
            for k in range(COLS):
                own[r * COLS + c, r * COLS + k] = tap(k - c)
            for j in range(4):
                sides[r * COLS + c, r * 4 + j] = tap(j - 4 - c)
                sides[r * COLS + c, 16 + r * 4 + j] = tap(COLS + j - c)
        for j in range(4):
            pick[r * 4 + j, r * COLS + j] = 1.0
            pick[16 + r * 4 + j, r * COLS + COLS - 4 + j] = 1.0
    seam = np.zeros((64, 320))
    for r in range(ROWS):
        for k in range(ROWS + 8):
            down = tap(k - 4 - r)
            for j in range(4):
                for edge in range(2):
                    seam[edge * 32 + r, k * 4 + j] = down * tap(j - 4 + 1 - edge)
                    seam[edge * 32 + r, 160 + k * 4 + j] = down * tap(j + 1 - edge)
    own_high, own_low = split(own)
    sides_high, sides_low = split(sides)
    blank = np.zeros((256, 64), ml_dtypes.bfloat16)
    first = np.concatenate([own_high, own_low, sides_high, sides_low, blank], axis=1)
    seam_high, seam_low = split(seam)
    second = np.zeros((96, 640), ml_dtypes.bfloat16)
    second[:64] = np.concatenate([seam_high, seam_low], axis=1)
    second[64:, :256] = pick.astype(ml_dtypes.bfloat16)
    wide = np.zeros((512, 256))
    for strip in range(4):
        for half in range(2):
            for c in range(COLS):
                for k in range(128):
                    wide[strip * 128 + half * COLS + c, half * 128 + k] = tap((strip - 1) * COLS + c - k)
    return first, second, np.concatenate(split(wide), axis=1)


def dot(a, b):
    return jnp.dot(a, b, preferred_element_type=F32)


def dot_nt(a, b):
    return lax.dot_general(a, b, (((1,), (1,)), ((), ())), preferred_element_type=F32)


def iota(shape, axis):
    return lax.broadcasted_iota(jnp.int32, shape, axis)


def rolled_tiles(tiles):
    return jnp.swapaxes(jnp.stack(tiles), 0, 1)


def join_strips(part, target):
    for j in range(N_MZ // 2):
        a, b = part[2 * j], part[2 * j + 1]
        at = slice(j * 128, (j + 1) * 128)
        target[:, 0:16, at] = jnp.concatenate([a[:, :, :64], b[:, :, :64]], axis=2)
        target[:, 16:32, at] = jnp.concatenate([a[:, :, 64:], b[:, :, 64:]], axis=2)


def produce_kernel(
    spectra, owner_in, peaks_in, pattern_index_in, patterns_in, blur_in, more_in, wide_in, done, last, score,
    owner, peaks, pattern_index, patterns, blur, more, wide, xs, pack_left, pack_right, left, right, ys, ion, coef,
    form, out, raw, land, rows_wide, joined, note, notes, total, totals,
    load_sem, halo_send, halo_recv, part_send, part_recv, part_own, rows_send, rows_recv, done_sem,
    note_send, note_recv, total_send, total_recv,
):
    pix, mz = lax.axis_index("pix"), lax.axis_index("mz")
    z, y = mz // SIDE, mz % SIDE

    def device(dp, dm):
        return {"pix": (pix + dp + N_PIX) % N_PIX, "mz": (mz + dm + N_MZ) % N_MZ}

    def peer(dz, dy):
        return ((z + dz) % SIDE) * SIDE + (y + dy) % SIDE

    def remote(src, dst, send, recv, target):
        return pltpu.make_async_remote_copy(
            src_ref=src, dst_ref=dst, send_sem=send, recv_sem=recv, device_id=target, device_id_type=MESH
        )

    def slot_of(g):
        return {0: 0, GROUPS + 1: 1}.get(g, g + 1)

    sources = [spectra, more_in, blur_in, owner_in, peaks_in, pattern_index_in, patterns_in, wide_in]
    targets = [xs.at[pl.ds(1, GROUPS)], more, blur, owner, peaks, pattern_index, patterns, wide]
    loads = [pltpu.make_async_copy(src, dst, load_sem.at[i]) for i, (src, dst) in enumerate(zip(sources, targets))]
    for copy in loads:
        copy.start()

    barrier = pltpu.get_barrier_semaphore()
    for dz, dy in ORDER:
        pl.semaphore_signal(barrier, inc=1, device_id={"mz": peer(dz, dy)}, device_id_type=MESH)
    for dp in (1, 7, 2, 3, 4, 5, 6):
        pl.semaphore_signal(barrier, inc=1, device_id=device(dp, 0), device_id_type=MESH)

    for copy in loads[:2]:
        copy.wait()
    pick = more[64:96, 0:256]

    def pack(g):
        ends = dot(pick, xs[g]).astype(BF16)
        pack_left[slot_of(g)] = ends[0:16]
        pack_right[slot_of(g)] = ends[16:32]

    for g in range(1, GROUPS + 1):
        pack(g)
    same = (iota((BINS, BINS), 0) == iota((BINS, BINS), 1)).astype(F32).astype(BF16)
    tiles = []
    for n in range(8):
        rows_here = [xs[1 + r // 4, (r % 4) * COLS : (r % 4 + 1) * COLS, :] for r in (2 * n, 2 * n + 16, 2 * n + 1, 2 * n + 17)]
        turned = dot_nt(same, jnp.concatenate(rows_here, axis=0)).astype(BF16)
        tiles += [turned[:, 0:128], turned[:, 128:256]]
    for d in range(N_MZ):
        out[0, d] = rolled_tiles([tile[d * 16 : (d + 1) * 16] for tile in tiles])

    pl.semaphore_wait(barrier, len(ORDER) + N_PIX - 1)

    inner, outer = pl.ds(2, GROUPS), pl.ds(0, 2)
    halo = [
        (xs.at[GROUPS], xs.at[0], (1, 0)),
        (xs.at[1], xs.at[GROUPS + 1], (-1, 0)),
        (pack_right.at[inner], left.at[inner], (0, 1)),
        (pack_left.at[inner], right.at[inner], (0, -1)),
        (pack_right.at[outer], left.at[outer], (0, 1)),
        (pack_left.at[outer], right.at[outer], (0, -1)),
    ]
    halo = [
        remote(src, dst, halo_send.at[i], halo_recv.at[i], device(*to)) for i, (src, dst, to) in enumerate(halo)
    ]
    for copy in halo[:4]:
        copy.start()

    def all_of(ref, sem, count):
        block = ref.at[pl.ds(0, count)]
        pltpu.make_async_copy(block, block, sem).wait()

    def wait_part(q, target):
        all_of(target, part_recv.at[q], len(ORDER))
        all_of(out.at[q], part_send.at[q], len(ORDER))
        pltpu.make_async_copy(out.at[q, mz], target.at[mz], part_own.at[q]).wait()

    def send(q, target, begin, end):
        copies = []
        order = list(enumerate(ORDER))
        for i, (dz, dy) in (order[::-1] if TURNED[q] else order)[begin:end]:
            to = peer(dz, dy)
            copies.append(remote(out.at[q, to], target.at[mz], part_send.at[q], part_recv.at[q], {"mz": to}))
        if begin == 0:
            copies.append(pltpu.make_async_copy(out.at[q, mz], target.at[mz], part_own.at[q]))
        for copy in copies:
            copy.start()

    send(0, raw, 0, 8)

    loads[2].wait()
    blur_high, blur_low, blur_sides = blur[:, 0:256], blur[:, 256:512], blur[:, 512:576]

    def columns_own(g):
        ys[g] = dot(blur_high, xs[g]) + dot(blur_low, xs[g])

    for g in range(1, GROUPS + 1):
        columns_own(g)

    for copy in loads[3:]:
        copy.wait()
    count = owner.shape[0]
    owner_row = owner[...].reshape(1, count)
    owner_hot = (iota((N_MZ, count), 0) == owner_row).astype(F32)
    before = (iota((count, count), 0) < iota((count, count), 1)).astype(F32).astype(BF16)
    earlier = dot(owner_hot.astype(BF16), before)
    rank = jnp.sum(earlier * owner_hot, axis=0, keepdims=True)
    slot = owner_row * CAP + rank.astype(jnp.int32)
    pattern_hot = (iota((patterns.shape[1], count), 0) == pattern_index[...].reshape(1, count)).astype(F32).astype(BF16)
    weight = dot(patterns[...].astype(BF16), pattern_hot)
    spread = jnp.zeros((BINS, count), F32)
    for k in range(peaks.shape[0]):
        spread += jnp.where(iota((BINS, count), 0) == peaks[k : k + 1, :], weight[k : k + 1, :], 0.0)
    spread = spread.astype(BF16)
    place = iota((256, count), 0)
    place = (place // 16) * CAP + place % 16
    for q in range(1, PARTS):
        slot_hot = (place + (q - 1) * 16 == slot).astype(F32).astype(BF16)
        coef[q - 1] = dot_nt(slot_hot, spread).astype(BF16)

    for copy in halo[:2]:
        copy.wait()

    @pl.when(pix == 0)
    def _():
        xs[0] = jnp.zeros(xs.shape[1:], BF16)

    @pl.when(pix == N_PIX - 1)
    def _():
        xs[GROUPS + 1] = jnp.zeros(xs.shape[1:], BF16)

    pack(0)
    pack(GROUPS + 1)
    for copy in halo[4:]:
        copy.start()
    send(0, raw, 8, 15)
    columns_own(0)
    columns_own(GROUPS + 1)
    for copy in halo[2:]:
        copy.wait()

    @pl.when(mz == 0)
    def _():
        left[...] = jnp.zeros(left.shape, BF16)

    @pl.when(mz == N_MZ - 1)
    def _():
        right[...] = jnp.zeros(right.shape, BF16)

    for g in range(GROUPS + 2):
        at = slot_of(g)
        sides = jnp.concatenate([left[at], right[at], left[at], right[at]], axis=0)
        ys[g] += dot(blur_sides, sides)

    edge = [ref[slot_of(g)] for ref in (left, pack_left) for g in range(GROUPS + 2)]
    edge = jnp.concatenate(edge, axis=0)
    ion[PIXELS + 64 : PIXELS + 128] = (dot(more[0:64, 0:320], edge) + dot(more[0:64, 320:640], edge)).astype(BF16)

    def rows(c, carry):
        for lanes in (slice(0, 128), slice(128, 256)):
            lines = [ys[k // 4, pl.ds(pl.multiple_of((k % 4) * COLS + c * 16, 16), 16), lanes] for k in range(ROWS + 7)]
            for r in range(-1, ROWS):
                result = taps[3] * lines[r + 4]
                for i in range(3):
                    result = result + taps[i] * (lines[r + 1 + i] + lines[r + 7 - i])
                at = PIXELS if r < 0 else (r % 16) * 128 + (r // 16) * 64
                ion[pl.ds(pl.multiple_of(at + c * 16, 16), 16), lanes] = result.astype(BF16)
        return carry

    lax.fori_loop(0, COLS // 16, rows, 0)

    def product(q):
        tiles = []
        for n in range(PIXELS // 256):
            result = dot_nt(coef[q - 1], ion[n * 256 : (n + 1) * 256, :]).astype(BF16)
            tiles += [result[:, 0:128], result[:, 128:256]]
        for j, tile in enumerate(tiles):
            form[q - 1, j] = tile
        form[q - 1, 16] = dot_nt(coef[q - 1], ion[PIXELS : PIXELS + 128, :]).astype(BF16)
        for d in range(N_MZ):
            out[q, d] = rolled_tiles([tile[d * 16 : (d + 1) * 16] for tile in tiles])

    product(1)
    send(1, land.at[0], 0, 8)
    product(2)
    product(3)

    lane, sub = iota((64, 128), 1), iota((8, 128), 0)
    keep_across = (lane % 64 != 0).astype(F32)
    keep_seam = jnp.where(mz > 0, (lane >= 96).astype(F32), 0.0)
    keep_top = jnp.where(pix > 0, 1.0, jnp.where(lane < 64, 0.0, 1.0))
    note[...] = jnp.zeros(note.shape, F32)

    for q in range(1, PARTS):
        def scores(d, carry, q=q):
            def value(j):
                return form[q - 1, j, pl.ds(pl.multiple_of(d * 64, 64), 64), :].astype(F32)

            extra = value(16)
            prior = jnp.where(lane < 64, extra, pltpu.roll(value(15), 64, 1))
            across = jnp.zeros((64, 128), F32)
            down = jnp.zeros((64, 128), F32)
            energy = jnp.zeros((64, 128), F32)
            for j in range(16):
                now = value(j)
                step = now - pltpu.roll(now, 1, 1)
                across += step * step
                step = now - prior
                if j == 0:
                    step = step * keep_top
                down += step * step
                energy += now * now
                prior = now
            step = extra - pltpu.roll(extra, 32, 1)
            rough = across * keep_across + down + step * step * keep_seam
            rough = jnp.sum(rough, axis=1, keepdims=True)
            energy = jnp.sum(energy, axis=1, keepdims=True)
            for k in range(4):
                acc = jnp.zeros((8, 128), F32)
                for half in range(2):
                    at = k * 16 + half * 8
                    base = sub + ((q - 1) * 16 + half * 8)
                    acc += jnp.where(lane[0:8] == base, rough[at : at + 8], 0.0)
                    acc += jnp.where(lane[0:8] == base + 64, energy[at : at + 8], 0.0)
                note[d * 4 + k] += jnp.sum(acc, axis=0, keepdims=True)
            return carry

        lax.fori_loop(0, N_MZ // 4, scores, 0)

    small = []
    for i, (dz, dy) in enumerate(ORDER):
        to = peer(dz, dy)
        small.append(remote(note.at[to], notes.at[mz], note_send, note_recv, {"mz": to}))
    for copy in small:
        copy.start()
    send(1, land.at[0], 8, 15)
    send(2, land.at[1], 0, 15)

    wait_part(0, raw)
    blank = jnp.zeros((256, 128), BF16)
    for j in range(N_MZ // 2):
        strips = [raw[k].reshape(256, 128) if 0 <= k < N_MZ else blank for k in range(2 * j - 1, 2 * j + 3)]
        strips = jnp.concatenate(strips, axis=1)
        result = (dot(strips, wide[:, 0:256]) + dot(strips, wide[:, 256:512])).reshape(16, 16, 256)
        rows_wide[:, 8:24, j * 128 : (j + 1) * 128] = result[:, :, 0:128]
        rows_wide[:, 24:40, j * 128 : (j + 1) * 128] = result[:, :, 128:256]
    above, below = pl.ds(0, 8), pl.ds(40, 8)
    edges = [
        remote(rows_wide.at[:, pl.ds(32, 8)], rows_wide.at[:, above], rows_send.at[0], rows_recv.at[0], device(1, 0)),
        remote(rows_wide.at[:, pl.ds(8, 8)], rows_wide.at[:, below], rows_send.at[1], rows_recv.at[1], device(-1, 0)),
    ]
    for copy in edges:
        copy.start()


    all_of(notes, note_recv, len(ORDER))
    all_of(note, note_send, len(ORDER))
    notes[mz] = note[mz]
    total[...] = jnp.sum(notes[...], axis=0)
    small = []
    for dp in range(1, N_PIX):
        to = device(dp, 0)
        small.append(remote(total, totals.at[pix], total_send, total_recv, to))
    for copy in small:
        copy.start()
    send(2, land.at[1], 15, 15)
    send(3, last, 0, 15)

    for copy in edges:
        copy.wait()

    @pl.when(pix == 0)
    def _():
        rows_wide[:, above, :] = jnp.zeros((16, 8, COLS * N_MZ), F32)

    @pl.when(pix == N_PIX - 1)
    def _():
        rows_wide[:, below, :] = jnp.zeros((16, 8, COLS * N_MZ), F32)

    def own_rows(b, carry):
        for j in range(N_MZ // 2):
            x = rows_wide[b, :, j * 128 : (j + 1) * 128]
            result = taps[3] * x[8:40]
            for i in range(3):
                result = result + taps[i] * (x[5 + i : 37 + i] + x[11 - i : 43 - i])
            joined[b, :, j * 128 : (j + 1) * 128] = result.astype(BF16)
        return carry

    lax.fori_loop(0, 16, own_rows, 0)
    stores = [pltpu.make_async_copy(joined.at[pl.ds(0, 16)], done.at[pl.ds(0, 16)], done_sem.at[0])]
    stores[0].start()

    all_of(totals, total_recv, N_PIX - 1)
    all_of(totals, total_send, N_PIX - 1)
    totals[pix] = total[...]
    final = jnp.sum(totals[...], axis=0)
    final = final / (pltpu.roll(final, 64, 1) + 1e-5)
    score[...] = jnp.broadcast_to(final, (8, 128))

    for q in (1, 2):
        wait_part(q, land.at[q - 1])
        at = pl.ds(q * 16, 16)
        join_strips(land.at[q - 1], joined.at[at])
        stores.append(pltpu.make_async_copy(joined.at[at], done.at[at], done_sem.at[q]))
        stores[q].start()
    for copy in stores:
        copy.wait()
    wait_part(3, last)


def place_kernel(done, last, score, ion_out, form_out, chaos_out, joined, sems):
    copies = [
        pltpu.make_async_copy(done.at[pl.ds(0, 16)], ion_out, sems.at[0]),
        pltpu.make_async_copy(done.at[pl.ds(16, 32)], form_out.at[pl.ds(0, 32)], sems.at[1]),
        pltpu.make_async_copy(joined, form_out.at[pl.ds(32, 16)], sems.at[2]),
    ]
    copies[0].start()
    copies[1].start()
    join_strips(last, joined)
    copies[2].start()
    chaos_out[...] = score[...]
    for copy in copies:
        copy.wait()


def body(spectra, owner, peaks, pattern_index, patterns):
    first, second, third = constants()
    dma = pltpu.SemaphoreType.DMA
    vmem, hbm, free = (pl.BlockSpec(memory_space=space) for space in (pltpu.VMEM, pltpu.HBM, pl.ANY))
    wide_cols = COLS * N_MZ
    inputs = (
        spectra.reshape(GROUPS, 256, BINS), owner, peaks.T, pattern_index, patterns.T,
        jnp.asarray(first), jnp.asarray(second), jnp.asarray(third),
    )
    inputs = [pltpu.with_memory_space_constraint(x, pltpu.HBM) for x in inputs]
    done, last, score = pl.pallas_call(
        produce_kernel,
        out_shape=(
            jax.ShapeDtypeStruct((48, ROWS, wide_cols), BF16),
            jax.ShapeDtypeStruct((N_MZ, 16, 16, 128), BF16),
            jax.ShapeDtypeStruct((8, 128), F32),
        ),
        in_specs=[hbm] * len(inputs),
        out_specs=(free, free, vmem),
        scratch_shapes=[pltpu.VMEM(x.shape, x.dtype) for x in inputs[1:]]
        + [
            pltpu.VMEM((GROUPS + 2, 256, BINS), BF16),
            pltpu.VMEM((GROUPS + 2, 16, BINS), BF16),
            pltpu.VMEM((GROUPS + 2, 16, BINS), BF16),
            pltpu.VMEM((GROUPS + 2, 16, BINS), BF16),
            pltpu.VMEM((GROUPS + 2, 16, BINS), BF16),
            pltpu.VMEM((GROUPS + 2, 256, BINS), F32),
            pltpu.VMEM((PIXELS + EXTRA, BINS), BF16),
            pltpu.VMEM((PARTS - 1, 256, BINS), BF16),
            pltpu.VMEM((PARTS - 1, 17, 256, 128), BF16),
            pltpu.VMEM((PARTS, N_MZ, 16, 16, 128), BF16),
            pltpu.VMEM((N_MZ, 16, 16, 128), BF16),
            pltpu.VMEM((2, N_MZ, 16, 16, 128), BF16),
            pltpu.VMEM((16, ROWS + 16, wide_cols), F32),
            pltpu.VMEM((48, ROWS, wide_cols), BF16),
            pltpu.VMEM((N_MZ, 1, 128), F32),
            pltpu.VMEM((N_MZ, 1, 128), F32),
            pltpu.VMEM((1, 128), F32),
            pltpu.VMEM((N_PIX, 1, 128), F32),
            dma((len(inputs),)),
            dma((6,)),
            dma((6,)),
            dma((PARTS,)),
            dma((PARTS,)),
            dma((PARTS,)),
            dma((2,)),
            dma((2,)),
            dma((3,)),
            dma,
            dma,
            dma,
            dma,
        ],
        compiler_params=pltpu.CompilerParams(
            collective_id=0, has_side_effects=True, vmem_limit_bytes=48 * 2**20
        ),
    )(*inputs)
    ion_images, formula_images, chaos = pl.pallas_call(
        place_kernel,
        out_shape=(
            jax.ShapeDtypeStruct((16, ROWS, wide_cols), BF16),
            jax.ShapeDtypeStruct((CAP, ROWS, wide_cols), BF16),
            jax.ShapeDtypeStruct((8, 128), F32),
        ),
        in_specs=[vmem, vmem, vmem],
        out_specs=(free, free, vmem),
        scratch_shapes=[pltpu.VMEM((16, ROWS, wide_cols), BF16), dma((3,))],
        compiler_params=pltpu.CompilerParams(vmem_limit_bytes=32 * 2**20),
    )(done, last, score)
    return ion_images, formula_images, chaos[0, :CAP]


def solution(mesh):
    in_specs = (P("pix", "mz", None), P(), P(), P(), P())
    out_specs = (P("mz", "pix", None), P("mz", "pix", None), P("mz"))
    return jax.shard_map(body, mesh=mesh, in_specs=in_specs, out_specs=out_specs, check_vma=False)
```

```python
import math

import jax
import jax.numpy as jnp
import ml_dtypes
import numpy as np
from jax import lax
from jax.experimental import pallas as pl
from jax.experimental.pallas import tpu as pltpu
from jax.sharding import PartitionSpec as P

MESH = pl.DeviceIdType.MESH
F32, BF16 = jnp.float32, jnp.bfloat16

CAP = 48
N_MZ, N_PIX = 16, 8
SIDE = 4
ROWS, COLS, BINS = 32, 64, 256
GROUPS = ROWS // 4
PIXELS = ROWS * COLS
EXTRA = 128
PARTS = 4
TURNED = (0, 0, 0, 1)

gauss_raw = [math.exp(-offset * offset / 4.5) for offset in range(-3, 4)]
taps = [value / sum(gauss_raw) for value in gauss_raw]

ORDER = [(0, 1), (1, 0), (0, 3), (3, 0), (1, 1), (3, 3), (1, 3), (3, 1), (2, 0), (0, 2), (2, 1), (1, 2), (2, 3), (3, 2), (2, 2)]


def tap(offset):
    return taps[offset + 3] if -3 <= offset <= 3 else 0.0


def split(matrix):
    high = matrix.astype(ml_dtypes.bfloat16)
    low = (matrix - high.astype(np.float64)).astype(ml_dtypes.bfloat16)
    return high, low


def constants():
    own = np.zeros((256, 256))
    sides = np.zeros((256, 32))
    pick = np.zeros((32, 256))
    for r in range(4):
        for c in range(COLS):
            for k in range(COLS):
                own[r * COLS + c, r * COLS + k] = tap(k - c)
            for j in range(4):
                sides[r * COLS + c, r * 4 + j] = tap(j - 4 - c)
                sides[r * COLS + c, 16 + r * 4 + j] = tap(COLS + j - c)
        for j in range(4):
            pick[r * 4 + j, r * COLS + j] = 1.0
            pick[16 + r * 4 + j, r * COLS + COLS - 4 + j] = 1.0
    seam = np.zeros((64, 320))
    for r in range(ROWS):
        for k in range(ROWS + 8):
            down = tap(k - 4 - r)
            for j in range(4):
                for edge in range(2):
                    seam[edge * 32 + r, k * 4 + j] = down * tap(j - 4 + 1 - edge)
                    seam[edge * 32 + r, 160 + k * 4 + j] = down * tap(j + 1 - edge)
    own_high, own_low = split(own)
    sides_high, sides_low = split(sides)
    blank = np.zeros((256, 64), ml_dtypes.bfloat16)
    first = np.concatenate([own_high, own_low, sides_high, sides_low, blank], axis=1)
    seam_high, seam_low = split(seam)
    second = np.zeros((96, 640), ml_dtypes.bfloat16)
    second[:64] = np.concatenate([seam_high, seam_low], axis=1)
    second[64:, :256] = pick.astype(ml_dtypes.bfloat16)
    wide = np.zeros((512, 256))
    for strip in range(4):
        for half in range(2):
            for c in range(COLS):
                for k in range(128):
                    wide[strip * 128 + half * COLS + c, half * 128 + k] = tap((strip - 1) * COLS + c - k)
    return first, second, np.concatenate(split(wide), axis=1)


def dot(a, b):
    return jnp.dot(a, b, preferred_element_type=F32)


def dot_nt(a, b):
    return lax.dot_general(a, b, (((1,), (1,)), ((), ())), preferred_element_type=F32)


def iota(shape, axis):
    return lax.broadcasted_iota(jnp.int32, shape, axis)


def rolled_tiles(tiles):
    return jnp.swapaxes(jnp.stack(tiles), 0, 1)


def join_strips(part, target):
    for j in range(N_MZ // 2):
        a, b = part[2 * j], part[2 * j + 1]
        at = slice(j * 128, (j + 1) * 128)
        target[:, 0:16, at] = jnp.concatenate([a[:, :, :64], b[:, :, :64]], axis=2)
        target[:, 16:32, at] = jnp.concatenate([a[:, :, 64:], b[:, :, 64:]], axis=2)


def produce_kernel(
    spectra, owner_in, peaks_in, pattern_index_in, patterns_in, blur_in, more_in, wide_in, done, last, score,
    owner, peaks, pattern_index, patterns, blur, more, wide, xs, pack_left, pack_right, left, right, ys, ion, coef,
    form, out, raw, land, rows_wide, joined, note, notes, total, totals,
    load_sem, halo_send, halo_recv, part_send, part_recv, part_own, rows_send, rows_recv, done_sem,
    note_send, note_recv, total_send, total_recv,
):
    pix, mz = lax.axis_index("pix"), lax.axis_index("mz")
    z, y = mz // SIDE, mz % SIDE

    def device(dp, dm):
        return {"pix": (pix + dp + N_PIX) % N_PIX, "mz": (mz + dm + N_MZ) % N_MZ}

    def peer(dz, dy):
        return ((z + dz) % SIDE) * SIDE + (y + dy) % SIDE

    def remote(src, dst, send, recv, target):
        return pltpu.make_async_remote_copy(
            src_ref=src, dst_ref=dst, send_sem=send, recv_sem=recv, device_id=target, device_id_type=MESH
        )

    def slot_of(g):
        return {0: 0, GROUPS + 1: 1}.get(g, g + 1)

    sources = [spectra, more_in, blur_in, owner_in, peaks_in, pattern_index_in, patterns_in, wide_in]
    targets = [xs.at[pl.ds(1, GROUPS)], more, blur, owner, peaks, pattern_index, patterns, wide]
    loads = [pltpu.make_async_copy(src, dst, load_sem.at[i]) for i, (src, dst) in enumerate(zip(sources, targets))]
    for copy in loads:
        copy.start()

    barrier = pltpu.get_barrier_semaphore()
    for dz, dy in ORDER:
        pl.semaphore_signal(barrier, inc=1, device_id={"mz": peer(dz, dy)}, device_id_type=MESH)
    for dp in (1, 7, 2, 3, 4, 5, 6):
        pl.semaphore_signal(barrier, inc=1, device_id=device(dp, 0), device_id_type=MESH)

    for copy in loads[:2]:
        copy.wait()
    pick = more[64:96, 0:256]

    def pack(g):
        ends = dot(pick, xs[g]).astype(BF16)
        pack_left[slot_of(g)] = ends[0:16]
        pack_right[slot_of(g)] = ends[16:32]

    for g in range(1, GROUPS + 1):
        pack(g)
    same = (iota((BINS, BINS), 0) == iota((BINS, BINS), 1)).astype(F32).astype(BF16)
    tiles = []
    for n in range(8):
        rows_here = [xs[1 + r // 4, (r % 4) * COLS : (r % 4 + 1) * COLS, :] for r in (2 * n, 2 * n + 16, 2 * n + 1, 2 * n + 17)]
        turned = dot_nt(same, jnp.concatenate(rows_here, axis=0)).astype(BF16)
        tiles += [turned[:, 0:128], turned[:, 128:256]]
    for d in range(N_MZ):
        out[0, d] = rolled_tiles([tile[d * 16 : (d + 1) * 16] for tile in tiles])

    pl.semaphore_wait(barrier, len(ORDER) + N_PIX - 1)

    inner, outer = pl.ds(2, GROUPS), pl.ds(0, 2)
    halo = [
        (xs.at[GROUPS], xs.at[0], (1, 0)),
        (xs.at[1], xs.at[GROUPS + 1], (-1, 0)),
        (pack_right.at[inner], left.at[inner], (0, 1)),
        (pack_left.at[inner], right.at[inner], (0, -1)),
        (pack_right.at[outer], left.at[outer], (0, 1)),
        (pack_left.at[outer], right.at[outer], (0, -1)),
    ]
    halo = [
        remote(src, dst, halo_send.at[i], halo_recv.at[i], device(*to)) for i, (src, dst, to) in enumerate(halo)
    ]
    for copy in halo[:4]:
        copy.start()

    def all_of(ref, sem, count):
        block = ref.at[pl.ds(0, count)]
        pltpu.make_async_copy(block, block, sem).wait()

    def wait_part(q, target):
        all_of(target, part_recv.at[q], len(ORDER))
        all_of(out.at[q], part_send.at[q], len(ORDER))
        pltpu.make_async_copy(out.at[q, mz], target.at[mz], part_own.at[q]).wait()

    def send(q, target, begin, end):
        copies = []
        order = list(enumerate(ORDER))
        for i, (dz, dy) in (order[::-1] if TURNED[q] else order)[begin:end]:
            to = peer(dz, dy)
            copies.append(remote(out.at[q, to], target.at[mz], part_send.at[q], part_recv.at[q], {"mz": to}))
        if begin == 0:
            copies.append(pltpu.make_async_copy(out.at[q, mz], target.at[mz], part_own.at[q]))
        for copy in copies:
            copy.start()

    send(0, raw, 0, 8)

    loads[2].wait()
    blur_high, blur_low, blur_sides = blur[:, 0:256], blur[:, 256:512], blur[:, 512:576]

    def columns_own(g):
        ys[g] = dot(blur_high, xs[g]) + dot(blur_low, xs[g])

    for g in range(1, GROUPS + 1):
        columns_own(g)

    for copy in loads[3:]:
        copy.wait()
    count = owner.shape[0]
    owner_row = owner[...].reshape(1, count)
    owner_hot = (iota((N_MZ, count), 0) == owner_row).astype(F32)
    before = (iota((count, count), 0) < iota((count, count), 1)).astype(F32).astype(BF16)
    earlier = dot(owner_hot.astype(BF16), before)
    rank = jnp.sum(earlier * owner_hot, axis=0, keepdims=True)
    slot = owner_row * CAP + rank.astype(jnp.int32)
    pattern_hot = (iota((patterns.shape[1], count), 0) == pattern_index[...].reshape(1, count)).astype(F32).astype(BF16)
    weight = dot(patterns[...].astype(BF16), pattern_hot)
    spread = jnp.zeros((BINS, count), F32)
    for k in range(peaks.shape[0]):
        spread += jnp.where(iota((BINS, count), 0) == peaks[k : k + 1, :], weight[k : k + 1, :], 0.0)
    spread = spread.astype(BF16)
    place = iota((256, count), 0)
    place = (place // 16) * CAP + place % 16
    for q in range(1, PARTS):
        slot_hot = (place + (q - 1) * 16 == slot).astype(F32).astype(BF16)
        coef[q - 1] = dot_nt(slot_hot, spread).astype(BF16)

    for copy in halo[:2]:
        copy.wait()

    @pl.when(pix == 0)
    def _():
        xs[0] = jnp.zeros(xs.shape[1:], BF16)

    @pl.when(pix == N_PIX - 1)
    def _():
        xs[GROUPS + 1] = jnp.zeros(xs.shape[1:], BF16)

    pack(0)
    pack(GROUPS + 1)
    for copy in halo[4:]:
        copy.start()
    send(0, raw, 8, 15)
    columns_own(0)
    columns_own(GROUPS + 1)
    for copy in halo[2:]:
        copy.wait()

    @pl.when(mz == 0)
    def _():
        left[...] = jnp.zeros(left.shape, BF16)

    @pl.when(mz == N_MZ - 1)
    def _():
        right[...] = jnp.zeros(right.shape, BF16)

    for g in range(GROUPS + 2):
        at = slot_of(g)
        sides = jnp.concatenate([left[at], right[at], left[at], right[at]], axis=0)
        ys[g] += dot(blur_sides, sides)

    edge = [ref[slot_of(g)] for ref in (left, pack_left) for g in range(GROUPS + 2)]
    edge = jnp.concatenate(edge, axis=0)
    ion[PIXELS + 64 : PIXELS + 128] = (dot(more[0:64, 0:320], edge) + dot(more[0:64, 320:640], edge)).astype(BF16)

    def rows(c, carry):
        for lanes in (slice(0, 128), slice(128, 256)):
            lines = [ys[k // 4, pl.ds(pl.multiple_of((k % 4) * COLS + c * 16, 16), 16), lanes] for k in range(ROWS + 7)]
            for r in range(-1, ROWS):
                result = taps[3] * lines[r + 4]
                for i in range(3):
                    result = result + taps[i] * (lines[r + 1 + i] + lines[r + 7 - i])
                at = PIXELS if r < 0 else (r % 16) * 128 + (r // 16) * 64
                ion[pl.ds(pl.multiple_of(at + c * 16, 16), 16), lanes] = result.astype(BF16)
        return carry

    lax.fori_loop(0, COLS // 16, rows, 0)

    def product(q):
        tiles = []
        for n in range(PIXELS // 256):
            result = dot_nt(coef[q - 1], ion[n * 256 : (n + 1) * 256, :]).astype(BF16)
            tiles += [result[:, 0:128], result[:, 128:256]]
        for j, tile in enumerate(tiles):
            form[q - 1, j] = tile
        form[q - 1, 16] = dot_nt(coef[q - 1], ion[PIXELS : PIXELS + 128, :]).astype(BF16)
        for d in range(N_MZ):
            out[q, d] = rolled_tiles([tile[d * 16 : (d + 1) * 16] for tile in tiles])

    product(1)
    send(1, land.at[0], 0, 8)
    product(2)
    product(3)

    lane, sub = iota((64, 128), 1), iota((8, 128), 0)
    keep_across = (lane % 64 != 0).astype(F32)
    keep_seam = jnp.where(mz > 0, (lane >= 96).astype(F32), 0.0)
    keep_top = jnp.where(pix > 0, 1.0, jnp.where(lane < 64, 0.0, 1.0))
    note[...] = jnp.zeros(note.shape, F32)

    for q in range(1, PARTS):
        def scores(d, carry, q=q):
            def value(j):
                return form[q - 1, j, pl.ds(pl.multiple_of(d * 64, 64), 64), :].astype(F32)

            extra = value(16)
            prior = jnp.where(lane < 64, extra, pltpu.roll(value(15), 64, 1))
            across = jnp.zeros((64, 128), F32)
            down = jnp.zeros((64, 128), F32)
            energy = jnp.zeros((64, 128), F32)
            for j in range(16):
                now = value(j)
                step = now - pltpu.roll(now, 1, 1)
                across += step * step
                step = now - prior
                if j == 0:
                    step = step * keep_top
                down += step * step
                energy += now * now
                prior = now
            step = extra - pltpu.roll(extra, 32, 1)
            rough = across * keep_across + down + step * step * keep_seam
            rough = jnp.sum(rough, axis=1, keepdims=True)
            energy = jnp.sum(energy, axis=1, keepdims=True)
            for k in range(4):
                acc = jnp.zeros((8, 128), F32)
                for half in range(2):
                    at = k * 16 + half * 8
                    base = sub + ((q - 1) * 16 + half * 8)
                    acc += jnp.where(lane[0:8] == base, rough[at : at + 8], 0.0)
                    acc += jnp.where(lane[0:8] == base + 64, energy[at : at + 8], 0.0)
                note[d * 4 + k] += jnp.sum(acc, axis=0, keepdims=True)
            return carry

        lax.fori_loop(0, N_MZ // 4, scores, 0)

    small = []
    for i, (dz, dy) in enumerate(ORDER):
        to = peer(dz, dy)
        small.append(remote(note.at[to], notes.at[mz], note_send, note_recv, {"mz": to}))
    for copy in small:
        copy.start()
    send(1, land.at[0], 8, 15)
    send(2, land.at[1], 0, 15)

    wait_part(0, raw)
    blank = jnp.zeros((256, 128), BF16)
    for j in range(N_MZ // 2):
        strips = [raw[k].reshape(256, 128) if 0 <= k < N_MZ else blank for k in range(2 * j - 1, 2 * j + 3)]
        strips = jnp.concatenate(strips, axis=1)
        result = (dot(strips, wide[:, 0:256]) + dot(strips, wide[:, 256:512])).reshape(16, 16, 256)
        rows_wide[:, 8:24, j * 128 : (j + 1) * 128] = result[:, :, 0:128]
        rows_wide[:, 24:40, j * 128 : (j + 1) * 128] = result[:, :, 128:256]
    above, below = pl.ds(0, 8), pl.ds(40, 8)
    edges = [
        remote(rows_wide.at[:, pl.ds(32, 8)], rows_wide.at[:, above], rows_send.at[0], rows_recv.at[0], device(1, 0)),
        remote(rows_wide.at[:, pl.ds(8, 8)], rows_wide.at[:, below], rows_send.at[1], rows_recv.at[1], device(-1, 0)),
    ]
    for copy in edges:
        copy.start()


    all_of(notes, note_recv, len(ORDER))
    all_of(note, note_send, len(ORDER))
    notes[mz] = note[mz]
    total[...] = jnp.sum(notes[...], axis=0)
    small = []
    for dp in range(1, N_PIX):
        to = device(dp, 0)
        small.append(remote(total, totals.at[pix], total_send, total_recv, to))
    for copy in small:
        copy.start()
    send(2, land.at[1], 15, 15)
    send(3, last, 0, 15)

    for copy in edges:
        copy.wait()

    @pl.when(pix == 0)
    def _():
        rows_wide[:, above, :] = jnp.zeros((16, 8, COLS * N_MZ), F32)

    @pl.when(pix == N_PIX - 1)
    def _():
        rows_wide[:, below, :] = jnp.zeros((16, 8, COLS * N_MZ), F32)

    def own_rows(b, carry):
        for j in range(N_MZ // 2):
            x = rows_wide[b, :, j * 128 : (j + 1) * 128]
            result = taps[3] * x[8:40]
            for i in range(3):
                result = result + taps[i] * (x[5 + i : 37 + i] + x[11 - i : 43 - i])
            joined[b, :, j * 128 : (j + 1) * 128] = result.astype(BF16)
        return carry

    lax.fori_loop(0, 16, own_rows, 0)
    stores = [pltpu.make_async_copy(joined.at[pl.ds(0, 16)], done.at[pl.ds(0, 16)], done_sem.at[0])]
    stores[0].start()

    all_of(totals, total_recv, N_PIX - 1)
    all_of(totals, total_send, N_PIX - 1)
    totals[pix] = total[...]
    final = jnp.sum(totals[...], axis=0)
    final = final / (pltpu.roll(final, 64, 1) + 1e-5)
    score[...] = jnp.broadcast_to(final, (8, 128))

    for q in (1, 2):
        wait_part(q, land.at[q - 1])
        at = pl.ds(q * 16, 16)
        join_strips(land.at[q - 1], joined.at[at])
        stores.append(pltpu.make_async_copy(joined.at[at], done.at[at], done_sem.at[q]))
        stores[q].start()
    for copy in stores:
        copy.wait()
    wait_part(3, last)


def place_kernel(done, last, score, ion_out, form_out, chaos_out, joined, chaos, sems):
    chaos[...] = score[0, 0:CAP]
    copies = [
        pltpu.make_async_copy(done.at[pl.ds(0, 16)], ion_out, sems.at[0]),
        pltpu.make_async_copy(done.at[pl.ds(16, 32)], form_out.at[pl.ds(0, 32)], sems.at[1]),
        pltpu.make_async_copy(chaos, chaos_out, sems.at[3]),
        pltpu.make_async_copy(joined, form_out.at[pl.ds(32, 16)], sems.at[2]),
    ]
    for copy in copies[:3]:
        copy.start()
    join_strips(last, joined)
    copies[3].start()
    for copy in copies:
        copy.wait()


def body(spectra, owner, peaks, pattern_index, patterns):
    first, second, third = constants()
    dma = pltpu.SemaphoreType.DMA
    vmem, hbm, free = (pl.BlockSpec(memory_space=space) for space in (pltpu.VMEM, pltpu.HBM, pl.ANY))
    wide_cols = COLS * N_MZ
    inputs = (
        spectra.reshape(GROUPS, 256, BINS), owner, peaks.T, pattern_index, patterns.T,
        jnp.asarray(first), jnp.asarray(second), jnp.asarray(third),
    )
    inputs = [pltpu.with_memory_space_constraint(x, pltpu.HBM) for x in inputs]
    done, last, score = pl.pallas_call(
        produce_kernel,
        out_shape=(
            jax.ShapeDtypeStruct((48, ROWS, wide_cols), BF16),
            jax.ShapeDtypeStruct((N_MZ, 16, 16, 128), BF16),
            jax.ShapeDtypeStruct((8, 128), F32),
        ),
        in_specs=[hbm] * len(inputs),
        out_specs=(free, free, vmem),
        scratch_shapes=[pltpu.VMEM(x.shape, x.dtype) for x in inputs[1:]]
        + [
            pltpu.VMEM((GROUPS + 2, 256, BINS), BF16),
            pltpu.VMEM((GROUPS + 2, 16, BINS), BF16),
            pltpu.VMEM((GROUPS + 2, 16, BINS), BF16),
            pltpu.VMEM((GROUPS + 2, 16, BINS), BF16),
            pltpu.VMEM((GROUPS + 2, 16, BINS), BF16),
            pltpu.VMEM((GROUPS + 2, 256, BINS), F32),
            pltpu.VMEM((PIXELS + EXTRA, BINS), BF16),
            pltpu.VMEM((PARTS - 1, 256, BINS), BF16),
            pltpu.VMEM((PARTS - 1, 17, 256, 128), BF16),
            pltpu.VMEM((PARTS, N_MZ, 16, 16, 128), BF16),
            pltpu.VMEM((N_MZ, 16, 16, 128), BF16),
            pltpu.VMEM((2, N_MZ, 16, 16, 128), BF16),
            pltpu.VMEM((16, ROWS + 16, wide_cols), F32),
            pltpu.VMEM((48, ROWS, wide_cols), BF16),
            pltpu.VMEM((N_MZ, 1, 128), F32),
            pltpu.VMEM((N_MZ, 1, 128), F32),
            pltpu.VMEM((1, 128), F32),
            pltpu.VMEM((N_PIX, 1, 128), F32),
            dma((len(inputs),)),
            dma((6,)),
            dma((6,)),
            dma((PARTS,)),
            dma((PARTS,)),
            dma((PARTS,)),
            dma((2,)),
            dma((2,)),
            dma((3,)),
            dma,
            dma,
            dma,
            dma,
        ],
        compiler_params=pltpu.CompilerParams(
            collective_id=0, has_side_effects=True, vmem_limit_bytes=48 * 2**20
        ),
    )(*inputs)
    ion_images, formula_images, chaos = pl.pallas_call(
        place_kernel,
        out_shape=(
            jax.ShapeDtypeStruct((16, ROWS, wide_cols), BF16),
            jax.ShapeDtypeStruct((CAP, ROWS, wide_cols), BF16),
            jax.ShapeDtypeStruct((CAP,), F32),
        ),
        in_specs=[vmem, vmem, vmem],
        out_specs=(free, free, free),
        scratch_shapes=[pltpu.VMEM((16, ROWS, wide_cols), BF16), pltpu.VMEM((CAP,), F32), dma((4,))],
        compiler_params=pltpu.CompilerParams(vmem_limit_bytes=32 * 2**20),
    )(done, last, score)
    return ion_images, formula_images, chaos


def solution(mesh):
    in_specs = (P("pix", "mz", None), P(), P(), P(), P())
    out_specs = (P("mz", "pix", None), P("mz", "pix", None), P("mz"))
    return jax.shard_map(body, mesh=mesh, in_specs=in_specs, out_specs=out_specs, check_vma=False)
```

```python
import math

import jax
import jax.numpy as jnp
import ml_dtypes
import numpy as np
from jax import lax
from jax.experimental import pallas as pl
from jax.experimental.pallas import tpu as pltpu
from jax.sharding import PartitionSpec as P

MESH = pl.DeviceIdType.MESH
F32, BF16 = jnp.float32, jnp.bfloat16

CAP = 48
N_MZ, N_PIX = 16, 8
SIDE = 4
ROWS, COLS, BINS = 32, 64, 256
GROUPS = ROWS // 4
PIXELS = ROWS * COLS
EXTRA = 128
PARTS = 4
TURNED = (0, 0, 0, 1)

gauss_raw = [math.exp(-offset * offset / 4.5) for offset in range(-3, 4)]
taps = [value / sum(gauss_raw) for value in gauss_raw]

ORDER = [(0, 1), (1, 0), (0, 3), (3, 0), (1, 1), (3, 3), (1, 3), (3, 1), (2, 0), (0, 2), (2, 1), (1, 2), (2, 3), (3, 2), (2, 2)]


def tap(offset):
    return taps[offset + 3] if -3 <= offset <= 3 else 0.0


def split(matrix):
    high = matrix.astype(ml_dtypes.bfloat16)
    low = (matrix - high.astype(np.float64)).astype(ml_dtypes.bfloat16)
    return high, low


def constants():
    own = np.zeros((256, 256))
    sides = np.zeros((256, 32))
    pick = np.zeros((32, 256))
    for r in range(4):
        for c in range(COLS):
            for k in range(COLS):
                own[r * COLS + c, r * COLS + k] = tap(k - c)
            for j in range(4):
                sides[r * COLS + c, r * 4 + j] = tap(j - 4 - c)
                sides[r * COLS + c, 16 + r * 4 + j] = tap(COLS + j - c)
        for j in range(4):
            pick[r * 4 + j, r * COLS + j] = 1.0
            pick[16 + r * 4 + j, r * COLS + COLS - 4 + j] = 1.0
    seam = np.zeros((64, 320))
    for r in range(ROWS):
        for k in range(ROWS + 8):
            down = tap(k - 4 - r)
            for j in range(4):
                for edge in range(2):
                    seam[edge * 32 + r, k * 4 + j] = down * tap(j - 4 + 1 - edge)
                    seam[edge * 32 + r, 160 + k * 4 + j] = down * tap(j + 1 - edge)
    own_high, own_low = split(own)
    sides_high, sides_low = split(sides)
    blank = np.zeros((256, 64), ml_dtypes.bfloat16)
    first = np.concatenate([own_high, own_low, sides_high, sides_low, blank], axis=1)
    seam_high, seam_low = split(seam)
    second = np.zeros((96, 640), ml_dtypes.bfloat16)
    second[:64] = np.concatenate([seam_high, seam_low], axis=1)
    second[64:, :256] = pick.astype(ml_dtypes.bfloat16)
    wide = np.zeros((512, 256))
    for strip in range(4):
        for half in range(2):
            for c in range(COLS):
                for k in range(128):
                    wide[strip * 128 + half * COLS + c, half * 128 + k] = tap((strip - 1) * COLS + c - k)
    return first, second, np.concatenate(split(wide), axis=1)


def dot(a, b):
    return jnp.dot(a, b, preferred_element_type=F32)


def dot_nt(a, b):
    return lax.dot_general(a, b, (((1,), (1,)), ((), ())), preferred_element_type=F32)


def iota(shape, axis):
    return lax.broadcasted_iota(jnp.int32, shape, axis)


def rolled_tiles(tiles):
    return jnp.swapaxes(jnp.stack(tiles), 0, 1)


def join_strips(part, target):
    for j in range(N_MZ // 2):
        a, b = part[2 * j], part[2 * j + 1]
        at = slice(j * 128, (j + 1) * 128)
        target[:, 0:16, at] = jnp.concatenate([a[:, :, :64], b[:, :, :64]], axis=2)
        target[:, 16:32, at] = jnp.concatenate([a[:, :, 64:], b[:, :, 64:]], axis=2)


def produce_kernel(
    spectra, owner_in, peaks_in, pattern_index_in, patterns_in, blur_in, more_in, wide_in, done, last, score,
    owner, peaks, pattern_index, patterns, blur, more, wide, xs, pack_left, pack_right, left, right, ys, ion, coef,
    form, out, raw, land, rows_wide, joined, note, notes, total, totals,
    load_sem, halo_send, halo_recv, part_send, part_recv, part_own, rows_send, rows_recv, done_sem,
    note_send, note_recv, total_send, total_recv,
):
    pix, mz = lax.axis_index("pix"), lax.axis_index("mz")
    z, y = mz // SIDE, mz % SIDE

    def device(dp, dm):
        return {"pix": (pix + dp + N_PIX) % N_PIX, "mz": (mz + dm + N_MZ) % N_MZ}

    def peer(dz, dy):
        return ((z + dz) % SIDE) * SIDE + (y + dy) % SIDE

    def remote(src, dst, send, recv, target):
        return pltpu.make_async_remote_copy(
            src_ref=src, dst_ref=dst, send_sem=send, recv_sem=recv, device_id=target, device_id_type=MESH
        )

    def slot_of(g):
        return {0: 0, GROUPS + 1: 1}.get(g, g + 1)

    sources = [spectra, more_in, blur_in, owner_in, peaks_in, pattern_index_in, patterns_in, wide_in]
    targets = [xs.at[pl.ds(1, GROUPS)], more, blur, owner, peaks, pattern_index, patterns, wide]
    loads = [pltpu.make_async_copy(src, dst, load_sem.at[i]) for i, (src, dst) in enumerate(zip(sources, targets))]
    for copy in loads:
        copy.start()

    barrier = pltpu.get_barrier_semaphore()
    for dz, dy in ORDER:
        pl.semaphore_signal(barrier, inc=1, device_id={"mz": peer(dz, dy)}, device_id_type=MESH)
    for dp in (1, 7, 2, 3, 4, 5, 6):
        pl.semaphore_signal(barrier, inc=1, device_id=device(dp, 0), device_id_type=MESH)

    for copy in loads[:2]:
        copy.wait()
    pick = more[64:96, 0:256]

    def pack(g):
        ends = dot(pick, xs[g]).astype(BF16)
        pack_left[slot_of(g)] = ends[0:16]
        pack_right[slot_of(g)] = ends[16:32]

    for g in range(1, GROUPS + 1):
        pack(g)
    same = (iota((BINS, BINS), 0) == iota((BINS, BINS), 1)).astype(F32).astype(BF16)
    tiles = []
    for n in range(8):
        rows_here = [xs[1 + r // 4, (r % 4) * COLS : (r % 4 + 1) * COLS, :] for r in (2 * n, 2 * n + 16, 2 * n + 1, 2 * n + 17)]
        turned = dot_nt(same, jnp.concatenate(rows_here, axis=0)).astype(BF16)
        tiles += [turned[:, 0:128], turned[:, 128:256]]
    for d in range(N_MZ):
        out[0, d] = rolled_tiles([tile[d * 16 : (d + 1) * 16] for tile in tiles])

    pl.semaphore_wait(barrier, len(ORDER) + N_PIX - 1)

    inner = pl.ds(2, GROUPS)
    top, bottom, head, foot = 0, 1, 2, GROUPS + 1
    halo = [
        (pack_right.at[inner], left.at[inner], (0, 1)),
        (pack_left.at[inner], right.at[inner], (0, -1)),
        (xs.at[GROUPS], xs.at[0], (1, 0)),
        (xs.at[1], xs.at[GROUPS + 1], (-1, 0)),
        (left.at[foot], left.at[top], (1, 0)),
        (right.at[foot], right.at[top], (1, 0)),
        (left.at[head], left.at[bottom], (-1, 0)),
        (right.at[head], right.at[bottom], (-1, 0)),
    ]
    halo = [
        remote(src, dst, halo_send.at[i], halo_recv.at[i], device(*to)) for i, (src, dst, to) in enumerate(halo)
    ]
    for copy in halo[:2]:
        copy.start()

    def all_of(ref, sem, count):
        block = ref.at[pl.ds(0, count)]
        pltpu.make_async_copy(block, block, sem).wait()

    def wait_part(q, target):
        all_of(target, part_recv.at[q], len(ORDER))
        all_of(out.at[q], part_send.at[q], len(ORDER))
        pltpu.make_async_copy(out.at[q, mz], target.at[mz], part_own.at[q]).wait()

    def send(q, target, begin, end):
        copies = []
        order = list(enumerate(ORDER))
        for i, (dz, dy) in (order[::-1] if TURNED[q] else order)[begin:end]:
            to = peer(dz, dy)
            copies.append(remote(out.at[q, to], target.at[mz], part_send.at[q], part_recv.at[q], {"mz": to}))
        if begin < end == 15:
            copies.append(pltpu.make_async_copy(out.at[q, mz], target.at[mz], part_own.at[q]))
        for copy in copies:
            copy.start()

    send(0, raw, 0, 2)
    for copy in halo[2:4]:
        copy.start()
    send(0, raw, 2, 5)

    loads[2].wait()
    blur_high, blur_low, blur_sides = blur[:, 0:256], blur[:, 256:512], blur[:, 512:576]

    def columns_own(g):
        ys[g] = dot(blur_high, xs[g]) + dot(blur_low, xs[g])

    for g in range(1, GROUPS + 1):
        columns_own(g)

    for copy in loads[3:]:
        copy.wait()
    count = owner.shape[0]
    owner_row = owner[...].reshape(1, count)
    owner_hot = (iota((N_MZ, count), 0) == owner_row).astype(F32)
    before = (iota((count, count), 0) < iota((count, count), 1)).astype(F32).astype(BF16)
    earlier = dot(owner_hot.astype(BF16), before)
    rank = jnp.sum(earlier * owner_hot, axis=0, keepdims=True)
    slot = owner_row * CAP + rank.astype(jnp.int32)
    pattern_hot = (iota((patterns.shape[1], count), 0) == pattern_index[...].reshape(1, count)).astype(F32).astype(BF16)
    weight = dot(patterns[...].astype(BF16), pattern_hot)
    spread = jnp.zeros((BINS, count), F32)
    for k in range(peaks.shape[0]):
        spread += jnp.where(iota((BINS, count), 0) == peaks[k : k + 1, :], weight[k : k + 1, :], 0.0)
    spread = spread.astype(BF16)
    place = iota((256, count), 0)
    place = (place // 16) * CAP + place % 16
    for q in range(1, PARTS):
        slot_hot = (place + (q - 1) * 16 == slot).astype(F32).astype(BF16)
        coef[q - 1] = dot_nt(slot_hot, spread).astype(BF16)

    for copy in halo[:2]:
        copy.wait()
    for copy in halo[4:]:
        copy.start()
    send(0, raw, 5, 15)
    for copy in halo[2:4]:
        copy.wait()

    @pl.when(pix == 0)
    def _():
        xs[0] = jnp.zeros(xs.shape[1:], BF16)

    @pl.when(pix == N_PIX - 1)
    def _():
        xs[GROUPS + 1] = jnp.zeros(xs.shape[1:], BF16)

    for g in (0, GROUPS + 1):
        columns_own(g)
        pack_left[slot_of(g)] = dot(pick[0:16], xs[g]).astype(BF16)
    for copy in halo[4:]:
        copy.wait()

    @pl.when(pix == 0)
    def _():
        left[top] = jnp.zeros(left.shape[1:], BF16)
        right[top] = jnp.zeros(right.shape[1:], BF16)

    @pl.when(pix == N_PIX - 1)
    def _():
        left[bottom] = jnp.zeros(left.shape[1:], BF16)
        right[bottom] = jnp.zeros(right.shape[1:], BF16)

    @pl.when(mz == 0)
    def _():
        left[...] = jnp.zeros(left.shape, BF16)

    @pl.when(mz == N_MZ - 1)
    def _():
        right[...] = jnp.zeros(right.shape, BF16)

    for g in range(GROUPS + 2):
        at = slot_of(g)
        sides = jnp.concatenate([left[at], right[at], left[at], right[at]], axis=0)
        ys[g] += dot(blur_sides, sides)

    edge = [ref[slot_of(g)] for ref in (left, pack_left) for g in range(GROUPS + 2)]
    edge = jnp.concatenate(edge, axis=0)
    ion[PIXELS + 64 : PIXELS + 128] = (dot(more[0:64, 0:320], edge) + dot(more[0:64, 320:640], edge)).astype(BF16)

    def rows(c, carry):
        for lanes in (slice(0, 128), slice(128, 256)):
            lines = [ys[k // 4, pl.ds(pl.multiple_of((k % 4) * COLS + c * 16, 16), 16), lanes] for k in range(ROWS + 7)]
            for r in range(-1, ROWS):
                result = taps[3] * lines[r + 4]
                for i in range(3):
                    result = result + taps[i] * (lines[r + 1 + i] + lines[r + 7 - i])
                at = PIXELS if r < 0 else (r % 16) * 128 + (r // 16) * 64
                ion[pl.ds(pl.multiple_of(at + c * 16, 16), 16), lanes] = result.astype(BF16)
        return carry

    lax.fori_loop(0, COLS // 16, rows, 0)

    def product(q):
        tiles = []
        for n in range(PIXELS // 256):
            result = dot_nt(coef[q - 1], ion[n * 256 : (n + 1) * 256, :]).astype(BF16)
            tiles += [result[:, 0:128], result[:, 128:256]]
        for j, tile in enumerate(tiles):
            form[q - 1, j] = tile
        form[q - 1, 16] = dot_nt(coef[q - 1], ion[PIXELS : PIXELS + 128, :]).astype(BF16)
        for d in range(N_MZ):
            out[q, d] = rolled_tiles([tile[d * 16 : (d + 1) * 16] for tile in tiles])

    product(1)
    send(1, land.at[0], 0, 11)
    product(2)
    product(3)

    lane, sub = iota((64, 128), 1), iota((8, 128), 0)
    keep_across = (lane % 64 != 0).astype(F32)
    keep_seam = jnp.where(mz > 0, (lane >= 96).astype(F32), 0.0)
    keep_top = jnp.where(pix > 0, 1.0, jnp.where(lane < 64, 0.0, 1.0))
    note[...] = jnp.zeros(note.shape, F32)

    for q in range(1, PARTS):
        def scores(d, carry, q=q):
            def value(j):
                return form[q - 1, j, pl.ds(pl.multiple_of(d * 64, 64), 64), :].astype(F32)

            extra = value(16)
            prior = jnp.where(lane < 64, extra, pltpu.roll(value(15), 64, 1))
            across = jnp.zeros((64, 128), F32)
            down = jnp.zeros((64, 128), F32)
            energy = jnp.zeros((64, 128), F32)
            for j in range(16):
                now = value(j)
                step = now - pltpu.roll(now, 1, 1)
                across += step * step
                step = now - prior
                if j == 0:
                    step = step * keep_top
                down += step * step
                energy += now * now
                prior = now
            step = extra - pltpu.roll(extra, 32, 1)
            rough = across * keep_across + down + step * step * keep_seam
            rough = jnp.sum(rough, axis=1, keepdims=True)
            energy = jnp.sum(energy, axis=1, keepdims=True)
            for k in range(4):
                acc = jnp.zeros((8, 128), F32)
                for half in range(2):
                    at = k * 16 + half * 8
                    base = sub + ((q - 1) * 16 + half * 8)
                    acc += jnp.where(lane[0:8] == base, rough[at : at + 8], 0.0)
                    acc += jnp.where(lane[0:8] == base + 64, energy[at : at + 8], 0.0)
                note[d * 4 + k] += jnp.sum(acc, axis=0, keepdims=True)
            return carry

        lax.fori_loop(0, N_MZ // 4, scores, 0)

    small = []
    for i, (dz, dy) in enumerate(ORDER):
        to = peer(dz, dy)
        small.append(remote(note.at[to], notes.at[mz], note_send, note_recv, {"mz": to}))
    for copy in small:
        copy.start()
    send(1, land.at[0], 11, 15)
    send(2, land.at[1], 0, 15)

    wait_part(0, raw)
    blank = jnp.zeros((256, 128), BF16)
    for j in range(N_MZ // 2):
        strips = [raw[k].reshape(256, 128) if 0 <= k < N_MZ else blank for k in range(2 * j - 1, 2 * j + 3)]
        strips = jnp.concatenate(strips, axis=1)
        result = (dot(strips, wide[:, 0:256]) + dot(strips, wide[:, 256:512])).reshape(16, 16, 256)
        rows_wide[:, 8:24, j * 128 : (j + 1) * 128] = result[:, :, 0:128]
        rows_wide[:, 24:40, j * 128 : (j + 1) * 128] = result[:, :, 128:256]
    above, below = pl.ds(0, 8), pl.ds(40, 8)
    edges = [
        remote(rows_wide.at[:, pl.ds(32, 8)], rows_wide.at[:, above], rows_send.at[0], rows_recv.at[0], device(1, 0)),
        remote(rows_wide.at[:, pl.ds(8, 8)], rows_wide.at[:, below], rows_send.at[1], rows_recv.at[1], device(-1, 0)),
    ]
    for copy in edges:
        copy.start()


    all_of(notes, note_recv, len(ORDER))
    all_of(note, note_send, len(ORDER))
    notes[mz] = note[mz]
    total[...] = jnp.sum(notes[...], axis=0)
    small = []
    for dp in range(1, N_PIX):
        to = device(dp, 0)
        small.append(remote(total, totals.at[pix], total_send, total_recv, to))
    for copy in small:
        copy.start()
    send(2, land.at[1], 15, 15)
    send(3, last, 0, 15)

    for copy in edges:
        copy.wait()

    @pl.when(pix == 0)
    def _():
        rows_wide[:, above, :] = jnp.zeros((16, 8, COLS * N_MZ), F32)

    @pl.when(pix == N_PIX - 1)
    def _():
        rows_wide[:, below, :] = jnp.zeros((16, 8, COLS * N_MZ), F32)

    def own_rows(b, carry):
        for j in range(N_MZ // 2):
            x = rows_wide[b, :, j * 128 : (j + 1) * 128]
            result = taps[3] * x[8:40]
            for i in range(3):
                result = result + taps[i] * (x[5 + i : 37 + i] + x[11 - i : 43 - i])
            joined[b, :, j * 128 : (j + 1) * 128] = result.astype(BF16)
        return carry

    lax.fori_loop(0, 16, own_rows, 0)
    stores = [pltpu.make_async_copy(joined.at[pl.ds(0, 16)], done.at[pl.ds(0, 16)], done_sem.at[0])]
    stores[0].start()

    all_of(totals, total_recv, N_PIX - 1)
    all_of(totals, total_send, N_PIX - 1)
    totals[pix] = total[...]
    final = jnp.sum(totals[...], axis=0)
    final = final / (pltpu.roll(final, 64, 1) + 1e-5)
    score[...] = jnp.broadcast_to(final, (8, 128))

    for q in (1, 2):
        wait_part(q, land.at[q - 1])
        at = pl.ds(q * 16, 16)
        join_strips(land.at[q - 1], joined.at[at])
        stores.append(pltpu.make_async_copy(joined.at[at], done.at[at], done_sem.at[q]))
        stores[q].start()
    for copy in stores:
        copy.wait()
    wait_part(3, last)


def place_kernel(done, last, score, ion_out, form_out, chaos_out, joined, chaos, sems):
    chaos[...] = score[0, 0:CAP]
    copies = [
        pltpu.make_async_copy(done.at[pl.ds(0, 16)], ion_out, sems.at[0]),
        pltpu.make_async_copy(done.at[pl.ds(16, 32)], form_out.at[pl.ds(0, 32)], sems.at[1]),
        pltpu.make_async_copy(chaos, chaos_out, sems.at[3]),
        pltpu.make_async_copy(joined, form_out.at[pl.ds(32, 16)], sems.at[2]),
    ]
    for copy in copies[:3]:
        copy.start()
    join_strips(last, joined)
    copies[3].start()
    for copy in copies:
        copy.wait()


def body(spectra, owner, peaks, pattern_index, patterns):
    first, second, third = constants()
    dma = pltpu.SemaphoreType.DMA
    vmem, hbm, free = (pl.BlockSpec(memory_space=space) for space in (pltpu.VMEM, pltpu.HBM, pl.ANY))
    wide_cols = COLS * N_MZ
    inputs = (
        spectra.reshape(GROUPS, 256, BINS), owner, peaks.T, pattern_index, patterns.T,
        jnp.asarray(first), jnp.asarray(second), jnp.asarray(third),
    )
    inputs = [pltpu.with_memory_space_constraint(x, pltpu.HBM) for x in inputs]
    done, last, score = pl.pallas_call(
        produce_kernel,
        out_shape=(
            jax.ShapeDtypeStruct((48, ROWS, wide_cols), BF16),
            jax.ShapeDtypeStruct((N_MZ, 16, 16, 128), BF16),
            jax.ShapeDtypeStruct((8, 128), F32),
        ),
        in_specs=[hbm] * len(inputs),
        out_specs=(free, free, vmem),
        scratch_shapes=[pltpu.VMEM(x.shape, x.dtype) for x in inputs[1:]]
        + [
            pltpu.VMEM((GROUPS + 2, 256, BINS), BF16),
            pltpu.VMEM((GROUPS + 2, 16, BINS), BF16),
            pltpu.VMEM((GROUPS + 2, 16, BINS), BF16),
            pltpu.VMEM((GROUPS + 2, 16, BINS), BF16),
            pltpu.VMEM((GROUPS + 2, 16, BINS), BF16),
            pltpu.VMEM((GROUPS + 2, 256, BINS), F32),
            pltpu.VMEM((PIXELS + EXTRA, BINS), BF16),
            pltpu.VMEM((PARTS - 1, 256, BINS), BF16),
            pltpu.VMEM((PARTS - 1, 17, 256, 128), BF16),
            pltpu.VMEM((PARTS, N_MZ, 16, 16, 128), BF16),
            pltpu.VMEM((N_MZ, 16, 16, 128), BF16),
            pltpu.VMEM((2, N_MZ, 16, 16, 128), BF16),
            pltpu.VMEM((16, ROWS + 16, wide_cols), F32),
            pltpu.VMEM((48, ROWS, wide_cols), BF16),
            pltpu.VMEM((N_MZ, 1, 128), F32),
            pltpu.VMEM((N_MZ, 1, 128), F32),
            pltpu.VMEM((1, 128), F32),
            pltpu.VMEM((N_PIX, 1, 128), F32),
            dma((len(inputs),)),
            dma((8,)),
            dma((8,)),
            dma((PARTS,)),
            dma((PARTS,)),
            dma((PARTS,)),
            dma((2,)),
            dma((2,)),
            dma((3,)),
            dma,
            dma,
            dma,
            dma,
        ],
        compiler_params=pltpu.CompilerParams(
            collective_id=0, has_side_effects=True, vmem_limit_bytes=48 * 2**20
        ),
    )(*inputs)
    ion_images, formula_images, chaos = pl.pallas_call(
        place_kernel,
        out_shape=(
            jax.ShapeDtypeStruct((16, ROWS, wide_cols), BF16),
            jax.ShapeDtypeStruct((CAP, ROWS, wide_cols), BF16),
            jax.ShapeDtypeStruct((CAP,), F32),
        ),
        in_specs=[vmem, vmem, vmem],
        out_specs=(free, free, free),
        scratch_shapes=[pltpu.VMEM((16, ROWS, wide_cols), BF16), pltpu.VMEM((CAP,), F32), dma((4,))],
        compiler_params=pltpu.CompilerParams(vmem_limit_bytes=32 * 2**20),
    )(done, last, score)
    return ion_images, formula_images, chaos


def solution(mesh):
    in_specs = (P("pix", "mz", None), P(), P(), P(), P())
    out_specs = (P("mz", "pix", None), P("mz", "pix", None), P("mz"))
    return jax.shard_map(body, mesh=mesh, in_specs=in_specs, out_specs=out_specs, check_vma=False)
```

```python
import math

import jax
import jax.numpy as jnp
import ml_dtypes
import numpy as np
from jax import lax
from jax.experimental import pallas as pl
from jax.experimental.pallas import tpu as pltpu
from jax.sharding import PartitionSpec as P

MESH = pl.DeviceIdType.MESH
F32, BF16 = jnp.float32, jnp.bfloat16

CAP = 48
N_MZ, N_PIX = 16, 8
SIDE = 4
ROWS, COLS, BINS = 32, 64, 256
GROUPS = ROWS // 4
PIXELS = ROWS * COLS
EXTRA = 128
PARTS = 4
TURNED = (0, 0, 0, 1)

gauss_raw = [math.exp(-offset * offset / 4.5) for offset in range(-3, 4)]
taps = [value / sum(gauss_raw) for value in gauss_raw]

ORDER = [(0, 1), (1, 0), (0, 3), (3, 0), (1, 1), (3, 3), (1, 3), (3, 1), (2, 0), (0, 2), (2, 1), (1, 2), (2, 3), (3, 2), (2, 2)]


def tap(offset):
    return taps[offset + 3] if -3 <= offset <= 3 else 0.0


def split(matrix):
    high = matrix.astype(ml_dtypes.bfloat16)
    low = (matrix - high.astype(np.float64)).astype(ml_dtypes.bfloat16)
    return high, low


def constants():
    own = np.zeros((256, 256))
    sides = np.zeros((256, 32))
    pick = np.zeros((32, 256))
    for r in range(4):
        for c in range(COLS):
            for k in range(COLS):
                own[r * COLS + c, r * COLS + k] = tap(k - c)
            for j in range(4):
                sides[r * COLS + c, r * 4 + j] = tap(j - 4 - c)
                sides[r * COLS + c, 16 + r * 4 + j] = tap(COLS + j - c)
        for j in range(4):
            pick[r * 4 + j, r * COLS + j] = 1.0
            pick[16 + r * 4 + j, r * COLS + COLS - 4 + j] = 1.0
    seam = np.zeros((64, 320))
    for r in range(ROWS):
        for k in range(ROWS + 8):
            down = tap(k - 4 - r)
            for j in range(4):
                for edge in range(2):
                    seam[edge * 32 + r, k * 4 + j] = down * tap(j - 4 + 1 - edge)
                    seam[edge * 32 + r, 160 + k * 4 + j] = down * tap(j + 1 - edge)
    own_high, own_low = split(own)
    sides_high, sides_low = split(sides)
    blank = np.zeros((256, 64), ml_dtypes.bfloat16)
    first = np.concatenate([own_high, own_low, sides_high, sides_low, blank], axis=1)
    seam_high, seam_low = split(seam)
    second = np.zeros((96, 640), ml_dtypes.bfloat16)
    second[:64] = np.concatenate([seam_high, seam_low], axis=1)
    second[64:, :256] = pick.astype(ml_dtypes.bfloat16)
    wide = np.zeros((512, 256))
    for strip in range(4):
        for half in range(2):
            for c in range(COLS):
                for k in range(128):
                    wide[strip * 128 + half * COLS + c, half * 128 + k] = tap((strip - 1) * COLS + c - k)
    return first, second, np.concatenate(split(wide), axis=1)


def dot(a, b):
    return jnp.dot(a, b, preferred_element_type=F32)


def dot_nt(a, b):
    return lax.dot_general(a, b, (((1,), (1,)), ((), ())), preferred_element_type=F32)


def iota(shape, axis):
    return lax.broadcasted_iota(jnp.int32, shape, axis)


def rolled_tiles(tiles):
    return jnp.swapaxes(jnp.stack(tiles), 0, 1)


def join_strips(part, target):
    for j in range(N_MZ // 2):
        a, b = part[2 * j], part[2 * j + 1]
        at = slice(j * 128, (j + 1) * 128)
        target[:, 0:16, at] = jnp.concatenate([a[:, :, :64], b[:, :, :64]], axis=2)
        target[:, 16:32, at] = jnp.concatenate([a[:, :, 64:], b[:, :, 64:]], axis=2)


def produce_kernel(
    spectra, owner_in, peaks_in, pattern_index_in, patterns_in, blur_in, more_in, wide_in, done, last, score,
    owner, peaks, pattern_index, patterns, blur, more, wide, xs, pack_left, pack_right, left, right, ys, ion, coef,
    form, out, raw, land, rows_wide, joined, note, notes, total, totals, score_here,
    load_sem, halo_send, halo_recv, part_send, part_recv, part_own, rows_send, rows_recv, done_sem,
    note_send, note_recv, total_send, total_recv,
):
    pix, mz = lax.axis_index("pix"), lax.axis_index("mz")
    z, y = mz // SIDE, mz % SIDE

    def device(dp, dm):
        return {"pix": (pix + dp + N_PIX) % N_PIX, "mz": (mz + dm + N_MZ) % N_MZ}

    def peer(dz, dy):
        return ((z + dz) % SIDE) * SIDE + (y + dy) % SIDE

    def remote(src, dst, send, recv, target):
        return pltpu.make_async_remote_copy(
            src_ref=src, dst_ref=dst, send_sem=send, recv_sem=recv, device_id=target, device_id_type=MESH
        )

    def slot_of(g):
        return {0: 0, GROUPS + 1: 1}.get(g, g + 1)

    sources = [spectra, more_in, blur_in, owner_in, peaks_in, pattern_index_in, patterns_in, wide_in]
    targets = [xs.at[pl.ds(1, GROUPS)], more, blur, owner, peaks, pattern_index, patterns, wide]
    loads = [pltpu.make_async_copy(src, dst, load_sem.at[i]) for i, (src, dst) in enumerate(zip(sources, targets))]
    for copy in loads[:2]:
        copy.start()

    barrier = pltpu.get_barrier_semaphore()
    for dz, dy in ORDER:
        pl.semaphore_signal(barrier, inc=1, device_id={"mz": peer(dz, dy)}, device_id_type=MESH)
    for dp in (1, 7, 2, 3, 4, 5, 6):
        pl.semaphore_signal(barrier, inc=1, device_id=device(dp, 0), device_id_type=MESH)

    for copy in loads[2:]:
        copy.start()

    for copy in loads[:2]:
        copy.wait()
    pick = more[64:96, 0:256]

    def pack(g):
        ends = dot(pick, xs[g]).astype(BF16)
        pack_left[slot_of(g)] = ends[0:16]
        pack_right[slot_of(g)] = ends[16:32]

    for g in range(1, GROUPS + 1):
        pack(g)
    same = (iota((BINS, BINS), 0) == iota((BINS, BINS), 1)).astype(F32).astype(BF16)
    tiles = []
    for n in range(8):
        rows_here = [xs[1 + r // 4, (r % 4) * COLS : (r % 4 + 1) * COLS, :] for r in (2 * n, 2 * n + 16, 2 * n + 1, 2 * n + 17)]
        turned = dot_nt(same, jnp.concatenate(rows_here, axis=0)).astype(BF16)
        tiles += [turned[:, 0:128], turned[:, 128:256]]
    for d in range(N_MZ):
        out[0, d] = rolled_tiles([tile[d * 16 : (d + 1) * 16] for tile in tiles])

    pl.semaphore_wait(barrier, len(ORDER) + N_PIX - 1)

    inner = pl.ds(2, GROUPS)
    top, bottom, head, foot = 0, 1, 2, GROUPS + 1
    halo = [
        (pack_right.at[inner], left.at[inner], (0, 1)),
        (pack_left.at[inner], right.at[inner], (0, -1)),
        (xs.at[GROUPS], xs.at[0], (1, 0)),
        (xs.at[1], xs.at[GROUPS + 1], (-1, 0)),
        (left.at[foot], left.at[top], (1, 0)),
        (right.at[foot], right.at[top], (1, 0)),
        (left.at[head], left.at[bottom], (-1, 0)),
        (right.at[head], right.at[bottom], (-1, 0)),
    ]
    halo = [
        remote(src, dst, halo_send.at[i], halo_recv.at[i], device(*to)) for i, (src, dst, to) in enumerate(halo)
    ]
    for copy in halo[:2]:
        copy.start()

    def all_of(ref, sem, count):
        block = ref.at[pl.ds(0, count)]
        pltpu.make_async_copy(block, block, sem).wait()

    def wait_part(q, target):
        all_of(target, part_recv.at[q], len(ORDER))
        all_of(out.at[q], part_send.at[q], len(ORDER))
        pltpu.make_async_copy(out.at[q, mz], target.at[mz], part_own.at[q]).wait()

    def send(q, target, begin, end):
        copies = []
        order = list(enumerate(ORDER))
        for i, (dz, dy) in (order[::-1] if TURNED[q] else order)[begin:end]:
            to = peer(dz, dy)
            copies.append(remote(out.at[q, to], target.at[mz], part_send.at[q], part_recv.at[q], {"mz": to}))
        if begin < end == 15:
            copies.append(pltpu.make_async_copy(out.at[q, mz], target.at[mz], part_own.at[q]))
        for copy in copies:
            copy.start()

    send(0, raw, 0, 2)
    for copy in halo[2:4]:
        copy.start()
    send(0, raw, 2, 5)

    loads[2].wait()
    blur_high, blur_low, blur_sides = blur[:, 0:256], blur[:, 256:512], blur[:, 512:576]

    def columns_own(g):
        ys[g] = dot(blur_high, xs[g]) + dot(blur_low, xs[g])

    for g in range(1, GROUPS + 1):
        columns_own(g)

    for copy in loads[3:]:
        copy.wait()
    count = owner.shape[0]
    owner_row = owner[...].reshape(1, count)
    owner_hot = (iota((N_MZ, count), 0) == owner_row).astype(F32)
    before = (iota((count, count), 0) < iota((count, count), 1)).astype(F32).astype(BF16)
    earlier = dot(owner_hot.astype(BF16), before)
    rank = jnp.sum(earlier * owner_hot, axis=0, keepdims=True)
    slot = owner_row * CAP + rank.astype(jnp.int32)
    pattern_hot = (iota((patterns.shape[1], count), 0) == pattern_index[...].reshape(1, count)).astype(F32).astype(BF16)
    weight = dot(patterns[...].astype(BF16), pattern_hot)
    spread = jnp.zeros((BINS, count), F32)
    for k in range(peaks.shape[0]):
        spread += jnp.where(iota((BINS, count), 0) == peaks[k : k + 1, :], weight[k : k + 1, :], 0.0)
    spread = spread.astype(BF16)
    place = iota((256, count), 0)
    place = (place // 16) * CAP + place % 16
    for q in range(1, PARTS):
        slot_hot = (place + (q - 1) * 16 == slot).astype(F32).astype(BF16)
        coef[q - 1] = dot_nt(slot_hot, spread).astype(BF16)

    for copy in halo[:2]:
        copy.wait()
    for copy in halo[4:]:
        copy.start()
    send(0, raw, 5, 15)
    for copy in halo[2:4]:
        copy.wait()

    @pl.when(pix == 0)
    def _():
        xs[0] = jnp.zeros(xs.shape[1:], BF16)

    @pl.when(pix == N_PIX - 1)
    def _():
        xs[GROUPS + 1] = jnp.zeros(xs.shape[1:], BF16)

    for g in (0, GROUPS + 1):
        columns_own(g)
        pack_left[slot_of(g)] = dot(pick[0:16], xs[g]).astype(BF16)
    for copy in halo[4:]:
        copy.wait()

    @pl.when(pix == 0)
    def _():
        left[top] = jnp.zeros(left.shape[1:], BF16)
        right[top] = jnp.zeros(right.shape[1:], BF16)

    @pl.when(pix == N_PIX - 1)
    def _():
        left[bottom] = jnp.zeros(left.shape[1:], BF16)
        right[bottom] = jnp.zeros(right.shape[1:], BF16)

    @pl.when(mz == 0)
    def _():
        left[...] = jnp.zeros(left.shape, BF16)

    @pl.when(mz == N_MZ - 1)
    def _():
        right[...] = jnp.zeros(right.shape, BF16)

    for g in range(GROUPS + 2):
        at = slot_of(g)
        sides = jnp.concatenate([left[at], right[at], left[at], right[at]], axis=0)
        ys[g] += dot(blur_sides, sides)

    edge = [ref[slot_of(g)] for ref in (left, pack_left) for g in range(GROUPS + 2)]
    edge = jnp.concatenate(edge, axis=0)
    ion[PIXELS + 64 : PIXELS + 128] = (dot(more[0:64, 0:320], edge) + dot(more[0:64, 320:640], edge)).astype(BF16)

    def rows(c, carry):
        for lanes in (slice(0, 128), slice(128, 256)):
            lines = [ys[k // 4, pl.ds(pl.multiple_of((k % 4) * COLS + c * 16, 16), 16), lanes] for k in range(ROWS + 7)]
            for r in range(-1, ROWS):
                result = taps[3] * lines[r + 4]
                for i in range(3):
                    result = result + taps[i] * (lines[r + 1 + i] + lines[r + 7 - i])
                at = PIXELS if r < 0 else (r % 16) * 128 + (r // 16) * 64
                ion[pl.ds(pl.multiple_of(at + c * 16, 16), 16), lanes] = result.astype(BF16)
        return carry

    lax.fori_loop(0, COLS // 16, rows, 0)

    def product(q):
        tiles = []
        for n in range(PIXELS // 256):
            result = dot_nt(coef[q - 1], ion[n * 256 : (n + 1) * 256, :]).astype(BF16)
            tiles += [result[:, 0:128], result[:, 128:256]]
        for j, tile in enumerate(tiles):
            form[q - 1, j] = tile
        form[q - 1, 16] = dot_nt(coef[q - 1], ion[PIXELS : PIXELS + 128, :]).astype(BF16)
        for d in range(N_MZ):
            out[q, d] = rolled_tiles([tile[d * 16 : (d + 1) * 16] for tile in tiles])

    product(1)
    send(1, land.at[0], 0, 11)
    product(2)
    product(3)

    lane, sub = iota((64, 128), 1), iota((8, 128), 0)
    keep_across = (lane % 64 != 0).astype(F32)
    keep_seam = jnp.where(mz > 0, (lane >= 96).astype(F32), 0.0)
    keep_top = jnp.where(pix > 0, 1.0, jnp.where(lane < 64, 0.0, 1.0))
    note[...] = jnp.zeros(note.shape, F32)

    for q in range(1, PARTS):
        def scores(d, carry, q=q):
            def value(j):
                return form[q - 1, j, pl.ds(pl.multiple_of(d * 64, 64), 64), :].astype(F32)

            extra = value(16)
            prior = jnp.where(lane < 64, extra, pltpu.roll(value(15), 64, 1))
            across = jnp.zeros((64, 128), F32)
            down = jnp.zeros((64, 128), F32)
            energy = jnp.zeros((64, 128), F32)
            for j in range(16):
                now = value(j)
                step = now - pltpu.roll(now, 1, 1)
                across += step * step
                step = now - prior
                if j == 0:
                    step = step * keep_top
                down += step * step
                energy += now * now
                prior = now
            step = extra - pltpu.roll(extra, 32, 1)
            rough = across * keep_across + down + step * step * keep_seam
            rough = jnp.sum(rough, axis=1, keepdims=True)
            energy = jnp.sum(energy, axis=1, keepdims=True)
            for k in range(4):
                acc = jnp.zeros((8, 128), F32)
                for half in range(2):
                    at = k * 16 + half * 8
                    base = sub + ((q - 1) * 16 + half * 8)
                    acc += jnp.where(lane[0:8] == base, rough[at : at + 8], 0.0)
                    acc += jnp.where(lane[0:8] == base + 64, energy[at : at + 8], 0.0)
                note[d * 4 + k] += jnp.sum(acc, axis=0, keepdims=True)
            return carry

        lax.fori_loop(0, N_MZ // 4, scores, 0)

    small = []
    for i, (dz, dy) in enumerate(ORDER):
        to = peer(dz, dy)
        small.append(remote(note.at[to], notes.at[mz], note_send, note_recv, {"mz": to}))
    for copy in small:
        copy.start()
    send(1, land.at[0], 11, 15)
    send(2, land.at[1], 0, 15)

    wait_part(0, raw)
    blank = jnp.zeros((256, 128), BF16)
    for j in range(N_MZ // 2):
        strips = [raw[k].reshape(256, 128) if 0 <= k < N_MZ else blank for k in range(2 * j - 1, 2 * j + 3)]
        strips = jnp.concatenate(strips, axis=1)
        result = (dot(strips, wide[:, 0:256]) + dot(strips, wide[:, 256:512])).reshape(16, 16, 256)
        rows_wide[:, 8:24, j * 128 : (j + 1) * 128] = result[:, :, 0:128]
        rows_wide[:, 24:40, j * 128 : (j + 1) * 128] = result[:, :, 128:256]
    above, below = pl.ds(0, 8), pl.ds(40, 8)
    edges = [
        remote(rows_wide.at[:, pl.ds(32, 8)], rows_wide.at[:, above], rows_send.at[0], rows_recv.at[0], device(1, 0)),
        remote(rows_wide.at[:, pl.ds(8, 8)], rows_wide.at[:, below], rows_send.at[1], rows_recv.at[1], device(-1, 0)),
    ]
    for copy in edges:
        copy.start()


    all_of(notes, note_recv, len(ORDER))
    all_of(note, note_send, len(ORDER))
    notes[mz] = note[mz]
    total[...] = jnp.sum(notes[...], axis=0)
    small = []
    for dp in range(1, N_PIX):
        to = device(dp, 0)
        small.append(remote(total, totals.at[pix], total_send, total_recv, to))
    for copy in small:
        copy.start()
    send(2, land.at[1], 15, 15)
    send(3, last, 0, 15)

    for copy in edges:
        copy.wait()

    @pl.when(pix == 0)
    def _():
        rows_wide[:, above, :] = jnp.zeros((16, 8, COLS * N_MZ), F32)

    @pl.when(pix == N_PIX - 1)
    def _():
        rows_wide[:, below, :] = jnp.zeros((16, 8, COLS * N_MZ), F32)

    def own_rows(b, carry):
        for j in range(N_MZ // 2):
            x = rows_wide[b, :, j * 128 : (j + 1) * 128]
            result = taps[3] * x[8:40]
            for i in range(3):
                result = result + taps[i] * (x[5 + i : 37 + i] + x[11 - i : 43 - i])
            joined[b, :, j * 128 : (j + 1) * 128] = result.astype(BF16)
        return carry

    lax.fori_loop(0, 16, own_rows, 0)
    stores = [pltpu.make_async_copy(joined.at[pl.ds(0, 16)], done.at[pl.ds(0, 16)], done_sem.at[0])]
    stores[0].start()

    all_of(totals, total_recv, N_PIX - 1)
    all_of(totals, total_send, N_PIX - 1)
    totals[pix] = total[...]
    final = jnp.sum(totals[...], axis=0)
    final = final / (pltpu.roll(final, 64, 1) + 1e-5)
    score_here[...] = jnp.broadcast_to(final, (8, 128))
    stores.append(pltpu.make_async_copy(score_here, score, done_sem.at[3]))
    stores[-1].start()

    for q in (1, 2):
        wait_part(q, land.at[q - 1])
        at = pl.ds(q * 16, 16)
        join_strips(land.at[q - 1], joined.at[at])
        stores.append(pltpu.make_async_copy(joined.at[at], done.at[at], done_sem.at[q]))
        stores[-1].start()
    for copy in stores:
        copy.wait()
    wait_part(3, last)


def place_kernel(done, last, score, ion_out, form_out, chaos_out, joined, chaos, sems):
    chaos[...] = score[0, 0:CAP]
    copies = [
        pltpu.make_async_copy(done.at[pl.ds(0, 16)], ion_out, sems.at[0]),
        pltpu.make_async_copy(done.at[pl.ds(16, 32)], form_out.at[pl.ds(0, 32)], sems.at[1]),
        pltpu.make_async_copy(chaos, chaos_out, sems.at[3]),
        pltpu.make_async_copy(joined, form_out.at[pl.ds(32, 16)], sems.at[2]),
    ]
    for copy in copies[:3]:
        copy.start()
    join_strips(last, joined)
    copies[3].start()
    for copy in copies:
        copy.wait()


def body(spectra, owner, peaks, pattern_index, patterns):
    first, second, third = constants()
    dma = pltpu.SemaphoreType.DMA
    vmem, hbm, free = (pl.BlockSpec(memory_space=space) for space in (pltpu.VMEM, pltpu.HBM, pl.ANY))
    wide_cols = COLS * N_MZ
    inputs = (
        spectra.reshape(GROUPS, 256, BINS), owner, peaks.T, pattern_index, patterns.T,
        jnp.asarray(first), jnp.asarray(second), jnp.asarray(third),
    )
    inputs = [pltpu.with_memory_space_constraint(x, pltpu.HBM) for x in inputs]
    done, last, score = pl.pallas_call(
        produce_kernel,
        out_shape=(
            jax.ShapeDtypeStruct((48, ROWS, wide_cols), BF16),
            jax.ShapeDtypeStruct((N_MZ, 16, 16, 128), BF16),
            jax.ShapeDtypeStruct((8, 128), F32),
        ),
        in_specs=[hbm] * len(inputs),
        out_specs=(free, free, free),
        scratch_shapes=[pltpu.VMEM(x.shape, x.dtype) for x in inputs[1:]]
        + [
            pltpu.VMEM((GROUPS + 2, 256, BINS), BF16),
            pltpu.VMEM((GROUPS + 2, 16, BINS), BF16),
            pltpu.VMEM((GROUPS + 2, 16, BINS), BF16),
            pltpu.VMEM((GROUPS + 2, 16, BINS), BF16),
            pltpu.VMEM((GROUPS + 2, 16, BINS), BF16),
            pltpu.VMEM((GROUPS + 2, 256, BINS), F32),
            pltpu.VMEM((PIXELS + EXTRA, BINS), BF16),
            pltpu.VMEM((PARTS - 1, 256, BINS), BF16),
            pltpu.VMEM((PARTS - 1, 17, 256, 128), BF16),
            pltpu.VMEM((PARTS, N_MZ, 16, 16, 128), BF16),
            pltpu.VMEM((N_MZ, 16, 16, 128), BF16),
            pltpu.VMEM((2, N_MZ, 16, 16, 128), BF16),
            pltpu.VMEM((16, ROWS + 16, wide_cols), F32),
            pltpu.VMEM((48, ROWS, wide_cols), BF16),
            pltpu.VMEM((N_MZ, 1, 128), F32),
            pltpu.VMEM((N_MZ, 1, 128), F32),
            pltpu.VMEM((1, 128), F32),
            pltpu.VMEM((N_PIX, 1, 128), F32),
            pltpu.VMEM((8, 128), F32),
            dma((len(inputs),)),
            dma((8,)),
            dma((8,)),
            dma((PARTS,)),
            dma((PARTS,)),
            dma((PARTS,)),
            dma((2,)),
            dma((2,)),
            dma((4,)),
            dma,
            dma,
            dma,
            dma,
        ],
        compiler_params=pltpu.CompilerParams(
            collective_id=0, has_side_effects=True, vmem_limit_bytes=48 * 2**20
        ),
    )(*inputs)
    ion_images, formula_images, chaos = pl.pallas_call(
        place_kernel,
        out_shape=(
            jax.ShapeDtypeStruct((16, ROWS, wide_cols), BF16),
            jax.ShapeDtypeStruct((CAP, ROWS, wide_cols), BF16),
            jax.ShapeDtypeStruct((CAP,), F32),
        ),
        in_specs=[vmem, vmem, vmem],
        out_specs=(free, free, free),
        scratch_shapes=[pltpu.VMEM((16, ROWS, wide_cols), BF16), pltpu.VMEM((CAP,), F32), dma((4,))],
        compiler_params=pltpu.CompilerParams(vmem_limit_bytes=32 * 2**20),
    )(done, last, score)
    return ion_images, formula_images, chaos


def solution(mesh):
    in_specs = (P("pix", "mz", None), P(), P(), P(), P())
    out_specs = (P("mz", "pix", None), P("mz", "pix", None), P("mz"))
    return jax.shard_map(body, mesh=mesh, in_specs=in_specs, out_specs=out_specs, check_vma=False)
```
